32 devices in a mesh: section: 2 (over core), dp: 16 (over z, y, x).
Axes of the slice: x: 2, y: 2, z: 4, core: 2. Of those that a mesh axis runs over, the one named last changes fastest.
Arguments:
- inputs: bfloat16 [2, 16, 1024, 512], P(None, 'dp'), may hold values from -6 to 6
- joined: int32 [2, 16], P(None, 'dp'), may hold values 0 or 1
- cotangent: bfloat16 [2, 16, 1024, 512], P(None, 'dp'), may hold values from -6 to 6
- gain_mix: bfloat16 [2, 512], P('section'), may hold values from 0.5 to 1.5
- conv_taps: bfloat16 [2, 4, 512], P('section'), may hold values from -1.5 to 1.5
- w_in: bfloat16 [2, 512, 2048], P('section'), may hold values from -0.5 to 0.5
- w_out: bfloat16 [2, 1024, 512], P('section'), may hold values from -0.1875 to 0.1875
- gain_mlp: bfloat16 [2, 512], P('section'), may hold values from 0.5 to 1.5
- w_up: bfloat16 [2, 512, 2048], P('section'), may hold values from -0.25 to 0.25
- w_down: bfloat16 [2, 2048, 512], P('section'), may hold values from -0.125 to 0.125
Outputs:
- layer_out: bfloat16 [2, 2, 16, 1024, 512], P('section', None, 'dp')
- input_grads: bfloat16 [2, 2, 16, 1024, 512], P('section', None, 'dp')
- grad_gain_mix: float32 [2, 512], P('section', 'dp')
- grad_conv: float32 [2, 4, 512], P('section', None, 'dp')
- grad_w_in: float32 [2, 512, 2048], P('section', 'dp')
- grad_w_out: float32 [2, 1024, 512], P('section', 'dp')
- grad_gain_mlp: float32 [2, 512], P('section', 'dp')
- grad_w_up: float32 [2, 512, 2048], P('section', 'dp')
- grad_w_down: float32 [2, 2048, 512], P('section', 'dp')
The draws below stay inside these ranges and needn't reach their ends.
All inputs are finite; a program needn't handle non-finite values. No bound on the sum of `joined` on one device may be relied on, other than what follows from the above.
Results may differ from the reference program's by a relative error of at most 0.007.
Values may be sent and summed in bfloat16 or wider, within the bound.
A program may use at most 256 MiB of HBM per device.

```python
import jax
import jax.numpy as jnp
from jax import lax

D = 512
H = 1024
FF = 2048
MB = 2
LEN = 1024
ROWS = 16


def shared_pattern(key):
    sign_key, tap_key = jax.random.split(key)
    sign_vector = jnp.where(jax.random.bernoulli(sign_key, 0.5, (D,)), 1.0, -1.0).astype(jnp.float32)
    tap_values = jnp.clip(0.5 * jax.random.normal(tap_key, (2, 4, D), jnp.float32), -1.5, 1.5)
    return (sign_vector, tap_values)


def draw_conv_taps(key, part):
    sign_vector, tap_values = shared_pattern(key)
    return tap_values.astype(jnp.bfloat16)


def draw_inputs(key, part):
    sign_vector, tap_values = shared_pattern(key)
    key = jax.random.fold_in(key, 23)
    full_shape = (MB, ROWS, LEN, D)
    noise_part = jax.random.normal(key, full_shape, jnp.float32)
    return jnp.clip(noise_part + sign_vector, -6.0, 6.0).astype(jnp.bfloat16)


def draw_w_in(key, part):
    sign_vector, tap_values = shared_pattern(key)
    key = jax.random.fold_in(key, 37)
    noise_key, rate_key = jax.random.split(key)
    noise_part = jnp.clip(jax.random.normal(noise_key, (2, D, 2 * H), jnp.float32), -4.0, 4.0) * D ** (-0.5)
    gate_depth = jax.random.uniform(rate_key, (2, 1, H), jnp.float32, 0.0, 6.0)
    layer_factor = jnp.array([1.4, 2.0], jnp.float32).reshape(2, 1, 1)
    direction = (sign_vector * jnp.sum(tap_values, axis=1))[:, :, None] / D
    gate_part = noise_part[:, :, :H] - gate_depth * layer_factor * direction
    combined = jnp.concatenate([gate_part, noise_part[:, :, H:]], axis=2)
    return jnp.clip(combined, -0.5, 0.5).astype(jnp.bfloat16)


def touch_ends(entries, stream_key, low, high):
    place = [jax.random.randint(jax.random.fold_in(stream_key, axis), (), 0, length) for axis, length in enumerate(entries.shape)]
    longest = entries.shape.index(max(entries.shape))
    next_to = place[:longest] + [(place[longest] + 1) % entries.shape[longest]] + place[longest + 1:]
    return entries.at[tuple(place)].set(low).at[tuple(next_to)].set(high)


def raised(values, rng, source, target, blocks, factor):
    def block_of(dim):
        return (jnp.arange(values.shape[dim]) // (values.shape[dim] // blocks)).reshape((-1,) + (1,) * (values.ndim - 1 - dim))

    one_side = jax.random.permutation(rng, blocks)[block_of(target)]
    other_side = (block_of(target) + blocks // 2) % blocks
    return jnp.where((block_of(source) == one_side) | (block_of(source) == other_side), factor * values, values)


def shard_levels(stream_key, extent, shards, low, top_value):
    loudness = 1.0
    for dim, parts in shards:
        draws = jax.random.uniform(jax.random.fold_in(jax.random.fold_in(stream_key, 6), dim), (parts,), jnp.float32, low / len(shards), top_value / len(shards))
        loudness = loudness * jnp.repeat(jnp.exp(draws), extent[dim] // parts).reshape((-1,) + (1,) * (len(extent) - 1 - dim))
    return loudness


def centred(key, dims, deviation, limit, cuts=(), held_as=jnp.bfloat16):
    drawn = jax.random.normal(key, dims, jnp.float32) * deviation
    if len(cuts) > 0:
        drawn = shard_levels(key, dims, cuts, -0.22, 0.18) * drawn
    return jnp.clip(drawn, min=-limit, max=limit).astype(held_as)


def gaussian_with(stream_key, shape, spread, limit, cuts, heavy, kind=jnp.bfloat16):
    drawn = spread * jax.random.normal(stream_key, shape, jnp.float32)
    if cuts:
        drawn = drawn * shard_levels(stream_key, shape, cuts, -0.22, 0.18)
    return jnp.clip(raised(drawn, jax.random.fold_in(stream_key, 3), *heavy), -limit, limit).astype(kind)


def setup_inputs(seed: int = 0) -> dict:
    arg_keys = jax.random.split(jax.random.key(seed), 11)
    inputs = draw_inputs(jax.random.fold_in(arg_keys[10], 71), 0)
    joined = touch_ends((jax.random.randint(arg_keys[1], (MB, ROWS), 0, 2) < 1).astype(jnp.int32), jax.random.fold_in(arg_keys[1], 1), 0, 1)
    cotangent = gaussian_with(arg_keys[2], (MB, ROWS, LEN, D), 1.0, 6.0, ((1, 16),), (1, 3, 16, 2.0))
    gain_mix = jnp.clip(1.0 + 0.1 * jax.random.normal(arg_keys[3], (2, D), jnp.float32), 0.5, 1.5).astype(jnp.bfloat16)
    conv_taps = draw_conv_taps(jax.random.fold_in(arg_keys[10], 71), 0)
    w_in = draw_w_in(jax.random.fold_in(arg_keys[10], 71), 0)
    w_out = centred(arg_keys[6], (2, H, D), H ** -0.5, 0.1875, ((0, 2),))
    gain_mlp = jnp.clip(1.0 + 0.1 * jax.random.normal(arg_keys[7], (2, D), jnp.float32), 0.5, 1.5).astype(jnp.bfloat16)
    w_up = centred(arg_keys[8], (2, D, FF), D ** -0.5, 0.25, ((0, 2),))
    w_down = centred(arg_keys[9], (2, FF, D), FF ** -0.5, 0.125, ((0, 2),))
    return dict(inputs=inputs, joined=joined, cotangent=cotangent, gain_mix=gain_mix, conv_taps=conv_taps, w_in=w_in, w_out=w_out, gain_mlp=gain_mlp, w_up=w_up, w_down=w_down)


@jax.custom_vjp
def low(v):
    return lax.optimization_barrier(v.astype(jnp.bfloat16)).astype(jnp.float32)

@jax.custom_vjp
def low_back(v):
    return v

def low_keep(v):
    return (low(v), None)

def low_pass(kept, grad):
    return (grad,)

def back_keep(v):
    return (v, None)

def back_low(kept, grad):
    return (low(grad),)
low.defvjp(low_keep, low_pass)
low_back.defvjp(back_keep, back_low)
epsilon = 1e-06

def root_norm(values, gain):
    return values * lax.rsqrt(lax.optimization_barrier(jnp.mean(values * values, axis=-1, keepdims=True)) + epsilon) * gain

def product(left, right):
    return jnp.dot(left, right, precision=lax.Precision.HIGHEST)

def combine(earlier, later_pair):
    return (earlier[0] * later_pair[0], later_pair[0] * earlier[1] + later_pair[1])

def layer_forward(sequence, linked, gain_mix, conv_taps, w_in, w_out, gain_mlp, w_up, w_down):
    length = sequence.shape[0]
    boundary = length // 2
    position = jnp.arange(length)
    normed = root_norm(sequence, gain_mix)
    conv_out = normed * conv_taps[0]
    for offset in range(1, 4):
        shifted = jnp.pad(normed, ((offset, 0), (0, 0)))[:length]
        crossing = (position >= boundary) & (position - offset < boundary)
        conv_out = conv_out + shifted * jnp.where(crossing, linked, 1.0)[:, None] * conv_taps[offset]
    conv_out = low(conv_out)
    projected = low_back(product(conv_out, w_in))
    hidden_width = w_out.shape[0]
    gate_logit = projected[:, :hidden_width]
    candidate = projected[:, hidden_width:]
    retain = jax.nn.sigmoid(-gate_logit) * jnp.where(position == boundary, linked, 1.0)[:, None]
    update = jax.nn.sigmoid(gate_logit) * jax.nn.softplus(candidate)
    _, states = lax.associative_scan(combine, (retain, update), axis=0)
    middle = sequence + low_back(product(low(states), w_out))
    normed_mlp = low(root_norm(middle, gain_mlp))
    pre_act = low_back(product(normed_mlp, w_up))
    activation = low(jax.nn.gelu(pre_act, approximate=True))
    return middle + low_back(product(activation, w_down))

def reference(inputs, joined, cotangent, gain_mix, conv_taps, w_in, w_out, gain_mlp, w_up, w_down):
    weights = [array.astype(jnp.float32) for array in (gain_mix, conv_taps, w_in, w_out, gain_mlp, w_up, w_down)]
    batches, row_count = joined.shape
    flat_inputs = inputs.astype(jnp.float32).reshape(batches * row_count, LEN, D)
    flat_linked = joined.astype(jnp.float32).reshape(batches * row_count)
    flat_cotangent = cotangent.astype(jnp.float32).reshape(batches * row_count, LEN, D)

    def per_row(running, element):
        sequence, linked, incoming = element

        def model(seq_in, between, layer_weights):
            lower = [weight[0] for weight in layer_weights]
            upper = [weight[1] for weight in layer_weights]
            middle = low_back(low(layer_forward(seq_in, linked, *lower))) + between
            return (layer_forward(middle, linked, *upper), middle)
        final, pullback, middle = jax.vjp(model, sequence, jnp.zeros_like(sequence), weights, has_aux=True)
        d_sequence, d_between, d_weights = pullback(incoming)
        running = [total_term + new_term for total_term, new_term in zip(running, d_weights)]
        return (running, (middle.astype(jnp.bfloat16), final.astype(jnp.bfloat16), d_sequence.astype(jnp.bfloat16), d_between.astype(jnp.bfloat16)))
    start = [jnp.zeros_like(weight) for weight in weights]
    totals, (middles, finals, d_sequences, d_middles) = lax.scan(per_row, start, (flat_inputs, flat_linked, flat_cotangent))
    full_shape = (batches, row_count, LEN, D)
    layer_out = jnp.stack([middles.reshape(full_shape), finals.reshape(full_shape)])
    input_grads = jnp.stack([d_sequences.reshape(full_shape), d_middles.reshape(full_shape)])
    return (layer_out, input_grads, totals[0], totals[1], totals[2], totals[3], totals[4], totals[5], totals[6])
```

```python
import jax
import jax.numpy as jnp
from jax import lax
from jax.experimental import pallas as pl
from jax.experimental.pallas import tpu as pltpu
from jax.sharding import PartitionSpec as P

f32 = jnp.float32
bf16 = jnp.bfloat16
epsilon = 1e-06
GROUP = 32
COLS = 256
GELU_A = 0.7978845608028654
GELU_B = GELU_A * 0.044715


def dot(left, right):
    return jnp.dot(left, right, preferred_element_type=f32)


def dot_nt(left, right):
    return lax.dot_general(left, right, (((1,), (1,)), ((), ())), preferred_element_type=f32)


def dot_tn(left, right):
    return lax.dot_general(left, right, (((0,), (0,)), ((), ())), preferred_element_type=f32)


def segment_rows(shape):
    return lax.broadcasted_iota(jnp.int32, shape, 0)


def entry_factor(shape, linked):
    row = segment_rows(shape)
    return jnp.where(row == 0, 0.0, jnp.where(row == GROUP // 2, linked, 1.0))


def exit_factor(shape, linked):
    row = segment_rows(shape)
    return jnp.where(row == GROUP - 1, 0.0, jnp.where(row == GROUP // 2 - 1, linked, 1.0))


def row_blocks(total, size):
    return [slice(start, start + size) for start in range(0, total, size)]


def inverse_norm(values):
    return lax.rsqrt(jnp.mean(values * values, axis=-1, keepdims=True) + epsilon)


def fold_rows(values):
    rows, width = values.shape
    return jnp.sum(values.reshape(rows // 8, 8, width), axis=0)


def logistic_pair(logit):
    small = jnp.exp(-jnp.abs(logit))
    large_side = 1.0 / (1.0 + small)
    small_side = small * large_side
    positive = logit >= 0
    return jnp.where(positive, large_side, small_side), jnp.where(positive, small_side, large_side)


def softplus_parts(value):
    small = jnp.exp(-jnp.abs(value))
    whole = 1.0 + small
    inverse = 1.0 / whole
    log_part = jnp.where(small < 2.0**-10, small * (1.0 - 0.5 * small), jnp.log(whole))
    slope = jnp.where(value >= 0, inverse, small * inverse)
    return jnp.maximum(value, 0.0) + log_part, slope


def gelu_parts(value):
    square = value * value
    inner = value * (GELU_A + GELU_B * square)
    half = 0.5 + 0.5 * jnp.tanh(inner)
    slope = half * (1.0 + (1.0 - half) * (value * (2.0 * GELU_A + 6.0 * GELU_B * square)))
    return (value * half).astype(bf16), slope.astype(bf16)


def forward_mix(linked, x, gain, taps, normed, conv):
    length = x.shape[0]
    lead = 3 * GROUP
    for rows in row_blocks(length, 128):
        values = x[rows].astype(f32)
        normed[lead + rows.start : lead + rows.stop] = values * inverse_norm(values) * gain[...]
    width = x.shape[1]
    factor = entry_factor((GROUP, width), linked)
    for back in range(1, 4):
        start = lead + length - back * GROUP
        block = normed[start : start + GROUP]
        normed[lead - back * GROUP : lead - (back - 1) * GROUP] = pltpu.roll(block, 1, 0) * factor
    for rows in row_blocks(length, 128):
        total = normed[lead + rows.start : lead + rows.stop] * taps[0:1]
        for back in range(1, 4):
            start = lead - back * GROUP + rows.start
            total = total + normed[start : start + 128] * taps[back : back + 1]
        conv[rows] = total.astype(bf16)


def forward_scan(linked, retain, update, states, states_low, cols):
    length = retain.shape[0]
    steps = length // GROUP
    shape = (GROUP, update.shape[1])
    ends = update[0:GROUP]
    spans = retain[0:GROUP, cols]
    for step in range(1, steps):
        rows = slice(step * GROUP, (step + 1) * GROUP)
        keep = retain[rows, cols]
        ends = keep * ends + update[rows]
        spans = keep * spans
    factor = entry_factor(shape, linked)
    spans = spans * factor
    row = segment_rows(shape)
    distance = 1
    while distance < GROUP:
        reach = jnp.where(row >= distance, spans, 0.0)
        ends = ends + reach * pltpu.roll(ends, distance, 0)
        spans = reach * pltpu.roll(spans, distance, 0)
        distance = 2 * distance
    carry = pltpu.roll(ends, 1, 0) * factor
    for step in range(steps):
        rows = slice(step * GROUP, (step + 1) * GROUP)
        carry = retain[rows, cols] * carry + update[rows]
        states[rows, cols] = carry
        states_low[rows, cols] = carry.astype(bf16)


def forward_gates(linked, conv, w_in, retain, update, states, states_low, slope, first):
    hidden = states.shape[1]
    for index in range(hidden // COLS):
        cols = slice(index * COLS, (index + 1) * COLS)
        far = slice(hidden + index * COLS, hidden + (index + 1) * COLS)
        opened, kept = logistic_pair(dot(conv[...], w_in[:, cols]))
        retain[:, cols] = kept
        soft, soft_slope = softplus_parts(dot(conv[...], w_in[:, far]))
        slope[:, cols] = (opened * soft_slope).astype(slope.dtype)
        part = update.at[index % 2]
        part[...] = opened * soft
        forward_scan(linked, retain, part, states, states_low, cols)


def forward_middle(x, states_low, w_out, gain, middle, normed_low):
    for rows in row_blocks(x.shape[0], 256):
        values = x[rows].astype(f32) + dot(states_low[rows], w_out[...])
        middle[rows] = values
        normed_low[rows] = (values * inverse_norm(values) * gain[...]).astype(bf16)


def forward_up(normed_low, w_up, act, act_slope):
    for cols in row_blocks(act.shape[1], COLS):
        act[:, cols], act_slope[:, cols] = gelu_parts(dot(normed_low[...], w_up[:, cols]))


def forward_down(middle, act, w_down, out):
    for rows in row_blocks(middle.shape[0], 256):
        out[rows] = (middle[rows] + dot(act[rows], w_down[...])).astype(bf16)


def backward_down(dy, act, act_slope, w_down, normed_t, d_pre, g_down, g_up):
    for cols in row_blocks(act.shape[1], COLS):
        d_act = dot_nt(dy[...], w_down[cols])
        d_pre[:, cols] = (d_act * act_slope[:, cols].astype(f32)).astype(bf16)
        g_down(cols, dot_tn(act[:, cols], dy[...]))
        g_up(cols, dot(normed_t[...], d_pre[:, cols]))


def backward_up(dy, d_pre, w_up, middle, gain, d_middle, d_middle_low):
    total = jnp.zeros((8, dy.shape[1]), f32)
    for rows in row_blocks(dy.shape[0], 256):
        d_normed = dot_nt(d_pre[rows], w_up[...])
        values = middle[rows]
        scale = inverse_norm(values)
        unit = values * scale
        total = total + fold_rows(d_normed * unit)
        d_unit = d_normed * gain[...]
        mean = jnp.mean(d_unit * unit, axis=-1, keepdims=True)
        result = dy[rows].astype(f32) + scale * (d_unit - unit * mean)
        d_middle[rows] = result
        d_middle_low[rows] = result.astype(bf16)
    return total


def backward_scan(linked, retain, states, slope, d_states, d_proj, cols, far):
    length = retain.shape[0]
    steps = length // GROUP
    shape = (GROUP, d_states.shape[1])
    last = slice(length - GROUP, length)
    running = d_states[last]
    spans = retain[last, cols]
    for step in range(steps - 2, -1, -1):
        rows = slice(step * GROUP, (step + 1) * GROUP)
        after = retain[(step + 1) * GROUP : (step + 2) * GROUP, cols]
        running = d_states[rows] + after * running
        spans = spans * retain[rows, cols]
    entry = entry_factor(shape, linked)
    ends = retain[0:GROUP, cols] * running * entry
    spans = spans * entry
    row = segment_rows(shape)
    distance = 1
    while distance < GROUP:
        reach = jnp.where(row < GROUP - distance, spans, 0.0)
        ends = ends + reach * pltpu.roll(ends, GROUP - distance, 0)
        spans = reach * pltpu.roll(spans, GROUP - distance, 0)
        distance = 2 * distance
    running = jnp.where(row < GROUP - 1, pltpu.roll(ends, GROUP - 1, 0), 0.0)
    first_before = pltpu.roll(states[last, cols], 1, 0) * entry
    for step in range(steps - 1, -1, -1):
        rows = slice(step * GROUP, (step + 1) * GROUP)
        running = d_states[rows] + running
        keep = retain[rows, cols]
        before = states[(step - 1) * GROUP : step * GROUP, cols] if step else first_before
        decayed = keep * running
        d_proj[rows, cols] = (decayed * (states[rows, cols] - before)).astype(bf16)
        d_proj[rows, far] = (running * slope[rows, cols].astype(f32)).astype(bf16)
        running = decayed


def backward_gates(linked, d_middle_low, w_out, retain, states, states_low, slope, conv_t, d_states, d_proj, g_out, g_in):
    hidden = states.shape[1]
    for index in range(hidden // COLS):
        cols = slice(index * COLS, (index + 1) * COLS)
        far = slice(hidden + index * COLS, hidden + (index + 1) * COLS)
        part = d_states.at[index % 2]
        part[...] = dot_nt(d_middle_low[...], w_out[cols])
        g_out(cols, dot_tn(states_low[:, cols], d_middle_low[...]))
        backward_scan(linked, retain, states, slope, part, d_proj, cols, far)
        g_in(cols, dot(conv_t[...], d_proj[:, cols]))
        g_in(far, dot(conv_t[...], d_proj[:, far]))


def backward_mix(linked, d_proj, w_in, x, gain, taps, d_middle, d_conv, out):
    length, width = x.shape
    for rows in row_blocks(length, 256):
        d_conv[rows] = dot_nt(d_proj[rows], w_in[...])
    factor = exit_factor((GROUP, width), linked)
    for ahead in range(3):
        block = d_conv[ahead * GROUP : (ahead + 1) * GROUP]
        d_conv[length + ahead * GROUP : length + (ahead + 1) * GROUP] = pltpu.roll(block, GROUP - 1, 0) * factor
    gain_total = jnp.zeros((8, width), f32)
    tap_totals = [jnp.zeros((8, width), f32) for _ in range(4)]
    for rows in row_blocks(length, 128):
        values = x[rows].astype(f32)
        scale = inverse_norm(values)
        unit = values * scale
        normed = unit * gain[...]
        d_normed = jnp.zeros_like(unit)
        for ahead in range(4):
            shifted = d_conv[rows.start + ahead * GROUP : rows.stop + ahead * GROUP]
            tap_totals[ahead] = tap_totals[ahead] + fold_rows(normed * shifted)
            d_normed = d_normed + shifted * taps[ahead : ahead + 1]
        gain_total = gain_total + fold_rows(d_normed * unit)
        d_unit = d_normed * gain[...]
        mean = jnp.mean(d_unit * unit, axis=-1, keepdims=True)
        out[rows] = (d_middle[rows] + scale * (d_unit - unit * mean)).astype(bf16)
    return gain_total, tap_totals


MESH = pl.DeviceIdType.MESH
GROUPS = 16


class Place:
    def __init__(self, per_group):
        self.core = lax.axis_index("section")
        index = lax.axis_index("dp")
        self.per_group = per_group
        self.inner = lax.rem(index, per_group)
        group = lax.div(index, per_group)
        self.line = lax.div(group, 4)
        high = lax.rem(lax.div(group, 2), 2)
        low = lax.rem(group, 2)
        self.first = low + self.core * (high - low)
        self.second = high + self.core * (low - high)

    def group(self, line, first, second):
        low = first + self.core * (second - first)
        high = second + self.core * (first - second)
        return line * 4 + high * 2 + low

    def device(self, line, first, second):
        return (self.core, self.group(line, first, second) * self.per_group + self.inner)

    def own(self):
        return self.group(self.line, self.first, self.second)

    def other_core(self):
        return (1 - self.core, lax.axis_index("dp"))

    def across_first(self):
        return self.device(self.line, 1 - self.first, self.second)

    def across_second(self):
        return self.device(self.line, self.first, 1 - self.second)

    def along(self, step):
        return lax.rem(self.line + step, 4)


def remote(source, target, sems, device):
    return pltpu.make_async_remote_copy(
        src_ref=source, dst_ref=target, send_sem=sems.at[0], recv_sem=sems.at[1], device_id=device, device_id_type=MESH
    )


def greet(place):
    barrier = pltpu.get_barrier_semaphore()
    others = [place.other_core(), place.across_first(), place.across_second()]
    others += [place.device(place.along(step), place.first, place.second) for step in range(1, 4)]
    for device in others:
        pl.semaphore_signal(barrier, inc=1, device_id=device, device_id_type=MESH)
    pl.semaphore_wait(barrier, len(others))


def send_first(place, own, landing, sems):
    for line in range(4):
        for second in range(2):
            source = own.at[place.group(line, 1 - place.first, second)]
            remote(source, landing.at[line * 2 + second], sems, place.across_first()).start()


def take_first(place, own, landing, sems):
    remote(landing, landing, sems, place.across_first()).wait()
    for line in range(4):
        for second in range(2):
            target = own.at[place.group(line, place.first, second)]
            target[...] = target[...] + landing[line * 2 + second]


def send_second(place, own, landing, sems):
    for line in range(4):
        source = own.at[place.group(line, place.first, 1 - place.second)]
        remote(source, landing.at[line], sems, place.across_second()).start()


def take_second(place, own, landing, sems):
    remote(landing, landing, sems, place.across_second()).wait()
    for line in range(4):
        target = own.at[place.group(line, place.first, place.second)]
        target[...] = target[...] + landing[line]


def send_line(place, own, landing, sems):
    for step in range(1, 4):
        line = place.along(step)
        source = own.at[place.group(line, place.first, place.second)]
        device = place.device(line, place.first, place.second)
        remote(source, landing.at[step - 1], sems, device).start()


def take_line(place, own, landing, sems):
    device = place.device(place.along(1), place.first, place.second)
    remote(landing, landing, sems, device).wait()
    total = own[place.own()].astype(f32)
    for step in range(3):
        total = total + landing[step].astype(f32)
    return total


VMEM = pl.BlockSpec(memory_space=pltpu.VMEM)
SMEM = pl.BlockSpec(memory_space=pltpu.SMEM)
LIMIT = 62 * 2**20


def forward_body(linked, x, gain_a, taps, w_in, w_out, gain_b, w_up, w_down, out, conv, retain, states, slope, low, middle, normed_low, act, act_slope, normed, update):
    joined = linked[0]
    forward_mix(joined, x, gain_a, taps, normed, conv)
    forward_gates(joined, conv, w_in, retain, update, states, low, slope, 0)
    forward_middle(x, low, w_out, gain_b, middle, normed_low)
    forward_up(normed_low, w_up, act, act_slope)
    forward_down(middle, act, w_down, out)


def forward(linked, x, gain_a, taps, w_in, w_out, gain_b, w_up, w_down):
    length, width = x.shape
    hidden, inner = w_out.shape[0], w_up.shape[1]
    shape = jax.ShapeDtypeStruct
    outs = [
        shape((length, width), bf16),
        shape((length, width), bf16),
        shape((length, hidden), f32),
        shape((length, hidden), f32),
        shape((length, hidden), bf16),
        shape((length, hidden), bf16),
        shape((length, width), f32),
        shape((length, width), bf16),
        shape((length, inner), bf16),
        shape((length, inner), bf16),
    ]
    args = (linked, x, gain_a, taps, w_in, w_out, gain_b, w_up, w_down)
    return pl.pallas_call(
        forward_body,
        out_shape=outs,
        in_specs=[SMEM] + [VMEM] * (len(args) - 1),
        out_specs=[VMEM] * len(outs),
        scratch_shapes=[pltpu.VMEM((length + 3 * GROUP, width), f32), pltpu.VMEM((2, length, COLS), f32)],
        compiler_params=pltpu.CompilerParams(vmem_limit_bytes=LIMIT),
        name="layer_forward",
    )(*args)


def backward_body(linked, x, gain_a, taps, w_in, w_out, gain_b, w_up, w_down, dy, conv, retain, states, slope, low, middle, normed_low, act, act_slope, dx, g_in, g_out, g_up, g_down, small, d_middle, d_middle_low, d_states, d_conv, turned, d_pre, d_proj):
    joined = linked[0]

    def rows_of(ref):
        def put(rows, values):
            ref[rows] = values.astype(bf16)

        return put

    def cols_of(ref):
        def put(cols, values):
            ref[:, cols] = values.astype(bf16)

        return put

    turned[...] = normed_low[...].T
    backward_down(dy, act, act_slope, w_down, turned, d_pre, rows_of(g_down), cols_of(g_up))
    mlp_total = backward_up(dy, d_pre, w_up, middle, gain_b, d_middle, d_middle_low)
    turned[...] = conv[...].T
    backward_gates(joined, d_middle_low, w_out, retain, states, low, slope, turned, d_states, d_proj, rows_of(g_out), cols_of(g_in))
    mix_total, tap_totals = backward_mix(joined, d_proj, w_in, x, gain_a, taps, d_middle, d_conv, dx)
    parts = [mix_total] + tap_totals + [mlp_total]
    small[...] = jnp.concatenate([jnp.sum(part, axis=0, keepdims=True) for part in parts] + [jnp.zeros((2, x.shape[1]), f32)], axis=0)


def backward(linked, x, gain_a, taps, w_in, w_out, gain_b, w_up, w_down, dy, *kept):
    length, width = x.shape
    hidden, inner = w_out.shape[0], w_up.shape[1]
    shape = jax.ShapeDtypeStruct
    outs = [
        shape((length, width), bf16),
        shape(w_in.shape, bf16),
        shape(w_out.shape, bf16),
        shape(w_up.shape, bf16),
        shape(w_down.shape, bf16),
        shape((8, width), f32),
    ]
    args = (linked, x, gain_a, taps, w_in, w_out, gain_b, w_up, w_down, dy) + tuple(kept)
    return pl.pallas_call(
        backward_body,
        out_shape=outs,
        in_specs=[SMEM] + [VMEM] * (len(args) - 1),
        out_specs=[VMEM] * len(outs),
        scratch_shapes=[
            pltpu.VMEM((length, width), f32),
            pltpu.VMEM((length, width), bf16),
            pltpu.VMEM((2, length, COLS), f32),
            pltpu.VMEM((length + 3 * GROUP, width), f32),
            pltpu.VMEM((width, length), bf16),
            pltpu.VMEM((length, inner), bf16),
            pltpu.VMEM((length, 2 * hidden), bf16),
        ],
        compiler_params=pltpu.CompilerParams(vmem_limit_bytes=LIMIT),
        name="layer_backward",
    )(*args)


def reduce_body(per_group, *refs):
    place = Place(per_group)
    grads, small, refs = refs[:8], refs[8], refs[9:]
    outs, small_out, refs = refs[:4], refs[4], refs[5:]
    own, landed, first, second, line, refs = refs[:8], refs[8:16], refs[16:24], refs[24:32], refs[32:40], refs[40:]
    result, arrived, refs = refs[:8], refs[8:12], refs[12:]
    small_land, sems, small_sems, last_sems = refs
    greet(place)
    halves = [own[unit].shape[2] for unit in range(8)]
    for unit in range(8):
        far = pl.ds(pl.multiple_of((1 - place.core) * halves[unit], halves[unit]), halves[unit])
        remote(grads[unit].at[:, :, far], landed[unit], sems.at[unit, 0], place.other_core()).start()
    small_copies = []

    def small_step(number, devices):
        copies = [
            remote(small_out, small_land.at[number + index], small_sems.at[number + index], device)
            for index, device in enumerate(devices)
        ]
        for copy in copies:
            copy.start()
        for copy in copies:
            copy.wait()
        total = small_out[...]
        for index in range(len(devices)):
            total = total + small_land[number + index]
        small_out[...] = total

    small_out[...] = small[...]
    small_step(0, [place.other_core()])
    for unit in range(8):
        near = pl.ds(pl.multiple_of(place.core * halves[unit], halves[unit]), halves[unit])
        remote(landed[unit], landed[unit], sems.at[unit, 0], place.other_core()).wait()
        own[unit][...] = grads[unit][:, :, near] + landed[unit][...]
        send_first(place, own[unit], first[unit], sems.at[unit, 1])
    small_step(1, [place.across_first()])
    for unit in range(8):
        take_first(place, own[unit], first[unit], sems.at[unit, 1])
        send_second(place, own[unit], second[unit], sems.at[unit, 2])
    small_step(2, [place.across_second()])
    for unit in range(8):
        take_second(place, own[unit], second[unit], sems.at[unit, 2])
        send_line(place, own[unit], line[unit], sems.at[unit, 3])
    small_step(3, [place.device(place.along(step), place.first, place.second) for step in range(1, 4)])
    for unit in range(8):
        result[unit][...] = take_line(place, own[unit], line[unit], sems.at[unit, 3])
    for piece in range(4):
        width = halves[piece]
        near = pl.ds(pl.multiple_of(place.core * width, width), width)
        far = pl.ds(pl.multiple_of((1 - place.core) * width, width), width)

        for layer in range(2):

            @pl.when(place.core == layer)
            def _():
                remote(result[(1 - layer) * 4 + piece], arrived[piece], last_sems.at[piece], place.other_core()).start()
                outs[piece][:, near] = result[layer * 4 + piece][...]

        remote(arrived[piece], arrived[piece], last_sems.at[piece], place.other_core()).wait()
        outs[piece][:, far] = arrived[piece][...]


def reduce_over_rows(per_group, grads, small):
    shape = jax.ShapeDtypeStruct
    shaped = [grad.reshape(GROUPS, grad.shape[0] // GROUPS, grad.shape[1]) for layer in grads for grad in layer]
    outs = [shape(grad.shape[1:], f32) for grad in shaped[:4]] + [shape(small.shape, f32)]

    def buffers(count, kind):
        return [
            pltpu.VMEM(((count,) if count else ()) + (grad.shape[1], grad.shape[2] // 2), kind) for grad in shaped
        ]

    scratch = buffers(GROUPS, bf16) + buffers(GROUPS, bf16) + buffers(8, bf16) + buffers(4, bf16) + buffers(3, bf16)
    scratch += buffers(0, f32) + buffers(0, f32)[:4]
    scratch += [
        pltpu.VMEM((6,) + small.shape, f32),
        pltpu.SemaphoreType.DMA((8, 4, 2)),
        pltpu.SemaphoreType.DMA((6, 2)),
        pltpu.SemaphoreType.DMA((4, 2)),
    ]
    return pl.pallas_call(
        lambda *refs: reduce_body(per_group, *refs),
        out_shape=outs,
        in_specs=[VMEM] * 9,
        out_specs=[VMEM] * 5,
        scratch_shapes=scratch,
        compiler_params=pltpu.CompilerParams(vmem_limit_bytes=LIMIT, collective_id=0, has_side_effects=True),
        name="reduce_rows",
    )(*shaped, small)


def swap_sections(block):
    return lax.ppermute(block, "section", [(0, 1), (1, 0)])


def local(inputs, joined, cotangent, gain_mix, conv_taps, w_in, w_out, gain_mlp, w_up, w_down):
    core = lax.axis_index("section")
    dp = lax.axis_size("dp")
    per_group = dp // GROUPS
    steps = inputs.shape[2] // GROUP

    def pick(pair):
        return lax.dynamic_index_in_dim(pair, core, 0, keepdims=False)

    def to_steps(block):
        return block.reshape(GROUP, steps, -1).swapaxes(0, 1).reshape(block.shape)

    def to_tokens(block):
        return block.reshape(steps, GROUP, -1).swapaxes(0, 1).reshape(block.shape)

    own_weights = (gain_mix, conv_taps, w_in, w_out, gain_mlp, w_up, w_down)
    layers = [[], []]
    for weight in own_weights:
        other = swap_sections(weight[0])
        layers[0].append(jnp.where(core == 0, weight[0], other))
        layers[1].append(jnp.where(core == 0, other, weight[0]))
    for layer in layers:
        layer[0] = layer[0][None].astype(f32)
        layer[1] = layer[1].astype(f32)
        layer[4] = layer[4][None].astype(f32)
    linked = pick(joined).astype(f32)
    x = to_steps(pick(inputs)[0])
    dy = to_steps(pick(cotangent)[0])
    y_first, *kept_first = forward(linked, x, *layers[0])
    y_second, *kept_second = forward(linked, y_first, *layers[1])
    dx_second, *grads_second = backward(linked, y_first, *layers[1], dy, *kept_second)
    dx_first, *grads_first = backward(linked, x, *layers[0], dx_second, *kept_first)

    def relay(of_first, of_second):
        of_first, of_second = to_tokens(of_first), to_tokens(of_second)
        kept = jnp.where(core == 0, of_first, of_second)
        moved = swap_sections(jnp.where(core == 0, of_second, of_first))
        return jnp.where(core == 0, jnp.stack([kept, moved]), jnp.stack([moved, kept]))[None, :, None]

    layer_out = relay(y_first, y_second)
    input_grads = relay(dx_first, dx_second)
    small = jnp.stack([grads_first[4], grads_second[4]])
    g_in, g_out, g_up, g_down, small = reduce_over_rows(per_group, [grads_first[:4], grads_second[:4]], small)
    small = pick(small)
    if per_group > 1:
        members = [[group * per_group + inner for inner in range(per_group)] for group in range(GROUPS)]

        def finish(grad):
            return lax.psum_scatter(grad, "dp", scatter_dimension=0, axis_index_groups=members, tiled=True)

        g_in, g_out, g_up, g_down = [finish(grad) for grad in (g_in, g_out, g_up, g_down)]
        small = lax.psum(small, "dp", axis_index_groups=members)
    lanes = small.shape[1] // dp
    small = lax.dynamic_slice_in_dim(small, lax.axis_index("dp") * lanes, lanes, 1)
    return (
        layer_out,
        input_grads,
        small[0:1],
        small[None, 1:5],
        g_in[None],
        g_out[None],
        small[5:6],
        g_up[None],
        g_down[None],
    )


def solution(mesh):
    placed = (
        P(None, "dp", None, None),
        P(None, "dp"),
        P(None, "dp", None, None),
        P("section", None),
        P("section", None, None),
        P("section", None, None),
        P("section", None, None),
        P("section", None),
        P("section", None, None),
        P("section", None, None),
    )
    return jax.shard_map(
        local,
        mesh=mesh,
        in_specs=placed,
        out_specs=(
            P("section", None, "dp", None, None),
            P("section", None, "dp", None, None),
            P("section", "dp"),
            P("section", None, "dp"),
            P("section", "dp", None),
            P("section", "dp", None),
            P("section", "dp"),
            P("section", "dp", None),
            P("section", "dp", None),
        ),
        check_vma=False,
    )
```

```python
import jax
import jax.numpy as jnp
from jax import lax
from jax.experimental import pallas as pl
from jax.experimental.pallas import tpu as pltpu
from jax.sharding import PartitionSpec as P

f32 = jnp.float32
bf16 = jnp.bfloat16
epsilon = 1e-06
GROUP = 32
COLS = 256
LANES = 128
GELU_A = 0.7978845608028654
GELU_B = GELU_A * 0.044715


def dot(left, right):
    return jnp.dot(left, right, preferred_element_type=f32)


def dot_nt(left, right):
    return lax.dot_general(left, right, (((1,), (1,)), ((), ())), preferred_element_type=f32)


def dot_tn(left, right):
    return lax.dot_general(left, right, (((0,), (0,)), ((), ())), preferred_element_type=f32)


def segment_rows(shape):
    return lax.broadcasted_iota(jnp.int32, shape, 0)


def entry_factor(shape, linked):
    row = segment_rows(shape)
    return jnp.where(row == 0, 0.0, jnp.where(row == GROUP // 2, linked, 1.0))


def exit_factor(shape, linked):
    row = segment_rows(shape)
    return jnp.where(row == GROUP - 1, 0.0, jnp.where(row == GROUP // 2 - 1, linked, 1.0))


def blocks(total, size):
    return [slice(start, start + size) for start in range(0, total, size)]


def inverse_norm(values):
    return lax.rsqrt(jnp.mean(values * values, axis=-1, keepdims=True) + epsilon)


def fold_rows(values):
    rows, width = values.shape
    return jnp.sum(values.reshape(rows // 8, 8, width), axis=0)


def logistic_pair(logit):
    small = jnp.exp(-jnp.abs(logit))
    large_side = 1.0 / (1.0 + small)
    small_side = small * large_side
    positive = logit >= 0
    return jnp.where(positive, large_side, small_side), jnp.where(positive, small_side, large_side)


def softplus_parts(value):
    small = jnp.exp(-jnp.abs(value))
    whole = 1.0 + small
    inverse = 1.0 / whole
    log_part = jnp.where(small < 2.0**-10, small * (1.0 - 0.5 * small), jnp.log(whole))
    slope = jnp.where(value >= 0, inverse, small * inverse)
    return jnp.maximum(value, 0.0) + log_part, slope


def gelu_parts(value):
    square = value * value
    inner = value * (GELU_A + GELU_B * square)
    half = 0.5 + 0.5 * jnp.tanh(inner)
    slope = half * (1.0 + (1.0 - half) * (value * (2.0 * GELU_A + 6.0 * GELU_B * square)))
    return (value * half).astype(bf16), slope.astype(bf16)


def swap_order(source, target, scratch):
    length, width = source.shape
    for tile in range(width // LANES):
        cols = slice(tile * LANES, (tile + 1) * LANES)
        scratch[tile] = source[:, cols].astype(f32)
    steps = length // GROUP
    for step in range(steps):
        rows = slice(step * GROUP, (step + 1) * GROUP)
        for tile in range(width // LANES):
            cols = slice(tile * LANES, (tile + 1) * LANES)
            target[rows, cols] = scratch[tile, pl.ds(step, GROUP, stride=steps), :].astype(bf16)


def forward_mix(linked, x, gain, taps, normed, conv):
    length, width = x.shape
    lead = 3 * GROUP
    for rows in blocks(length, 128):
        values = x[rows].astype(f32)
        normed[lead + rows.start : lead + rows.stop] = values * inverse_norm(values) * gain
    factor = entry_factor((GROUP, width), linked)
    for back in range(1, 4):
        start = lead + length - back * GROUP
        block = normed[start : start + GROUP]
        normed[lead - back * GROUP : lead - (back - 1) * GROUP] = pltpu.roll(block, 1, 0) * factor
    for rows in blocks(length, 128):
        total = normed[lead + rows.start : lead + rows.stop] * taps[0]
        for back in range(1, 4):
            start = lead - back * GROUP + rows.start
            total = total + normed[start : start + 128] * taps[back]
        conv[rows] = total.astype(bf16)


def forward_scan(linked, retain, update, states, states_low, cols):
    length = retain.shape[0]
    steps = length // GROUP
    shape = (GROUP, LANES)
    ends = update[0:GROUP]
    spans = retain[0:GROUP, cols]
    for step in range(1, steps):
        rows = slice(step * GROUP, (step + 1) * GROUP)
        keep = retain[rows, cols]
        ends = keep * ends + update[rows]
        spans = keep * spans
    factor = entry_factor(shape, linked)
    spans = spans * factor
    row = segment_rows(shape)
    distance = 1
    while distance < GROUP:
        reach = jnp.where(row >= distance, spans, 0.0)
        ends = ends + reach * pltpu.roll(ends, distance, 0)
        spans = reach * pltpu.roll(spans, distance, 0)
        distance = 2 * distance
    carry = pltpu.roll(ends, 1, 0) * factor
    for step in range(steps):
        rows = slice(step * GROUP, (step + 1) * GROUP)
        carry = retain[rows, cols] * carry + update[rows]
        states[rows, cols] = carry
        states_low[rows, cols] = carry.astype(bf16)


def forward_gates(linked, conv, w_in, retain, update, states, states_low, slope, index):
    hidden = states.shape[1]
    cols = slice(index * COLS, (index + 1) * COLS)
    far = slice(hidden + index * COLS, hidden + (index + 1) * COLS)
    opened, kept = logistic_pair(dot(conv[...], w_in[:, cols]))
    retain[:, cols] = kept
    soft, soft_slope = softplus_parts(dot(conv[...], w_in[:, far]))
    slope[:, cols] = (opened * soft_slope).astype(bf16)
    added = opened * soft
    for half in range(COLS // LANES):
        part = update.at[(index % 2) * (COLS // LANES) + half]
        part[...] = added[:, half * LANES : (half + 1) * LANES]
        lanes = slice(cols.start + half * LANES, cols.start + (half + 1) * LANES)
        forward_scan(linked, retain, part, states, states_low, lanes)


def forward_middle(x, states_low, w_out, gain, middle, normed_low):
    hidden = w_out.shape[0]
    for rows in blocks(x.shape[0], 256):
        values = x[rows].astype(f32) + dot(states_low[rows, 0:hidden], w_out[...])
        middle[rows] = values
        normed_low[rows] = (values * inverse_norm(values) * gain).astype(bf16)


def forward_up(normed_low, w_up, act, act_slope):
    for cols in blocks(act.shape[1], COLS):
        act[:, cols], act_slope[:, cols] = gelu_parts(dot(normed_low[...], w_up[:, cols]))


def forward_down(middle, act, w_down, out):
    for rows in blocks(middle.shape[0], 256):
        out[rows] = (middle[rows] + dot(act[rows], w_down[...])).astype(bf16)


def backward_up(dy, d_pre, w_up, middle, gain, d_middle, d_middle_low):
    total = jnp.zeros((8, dy.shape[1]), f32)
    for rows in blocks(dy.shape[0], 256):
        d_normed = dot_nt(d_pre[rows], w_up[...])
        values = middle[rows]
        scale = inverse_norm(values)
        unit = values * scale
        total = total + fold_rows(d_normed * unit)
        d_unit = d_normed * gain
        mean = jnp.mean(d_unit * unit, axis=-1, keepdims=True)
        result = dy[rows].astype(f32) + scale * (d_unit - unit * mean)
        d_middle[rows] = result
        d_middle_low[rows] = result.astype(bf16)
    return total


def backward_scan(linked, retain, states, slope, d_states, d_proj, cols, far):
    length = retain.shape[0]
    steps = length // GROUP
    shape = (GROUP, LANES)
    last = slice(length - GROUP, length)
    running = d_states[last]
    spans = retain[last, cols]
    for step in range(steps - 2, -1, -1):
        rows = slice(step * GROUP, (step + 1) * GROUP)
        after = retain[(step + 1) * GROUP : (step + 2) * GROUP, cols]
        running = d_states[rows] + after * running
        spans = spans * retain[rows, cols]
    entry = entry_factor(shape, linked)
    ends = retain[0:GROUP, cols] * running * entry
    spans = spans * entry
    row = segment_rows(shape)
    distance = 1
    while distance < GROUP:
        reach = jnp.where(row < GROUP - distance, spans, 0.0)
        ends = ends + reach * pltpu.roll(ends, GROUP - distance, 0)
        spans = reach * pltpu.roll(spans, GROUP - distance, 0)
        distance = 2 * distance
    running = jnp.where(row < GROUP - 1, pltpu.roll(ends, GROUP - 1, 0), 0.0)
    first_before = pltpu.roll(states[last, cols], 1, 0) * entry
    for step in range(steps - 1, -1, -1):
        rows = slice(step * GROUP, (step + 1) * GROUP)
        running = d_states[rows] + running
        keep = retain[rows, cols]
        before = states[(step - 1) * GROUP : step * GROUP, cols] if step else first_before
        decayed = keep * running
        d_proj[rows, cols] = (decayed * (states[rows, cols] - before)).astype(bf16)
        d_proj[rows, far] = (running * slope[rows, cols].astype(f32)).astype(bf16)
        running = decayed


def backward_gates(linked, d_middle_low, w_out, retain, states, slope, d_states, d_proj, index):
    hidden = states.shape[1]
    cols = slice(index * COLS, (index + 1) * COLS)
    d_hidden = dot_nt(d_middle_low[...], w_out[cols])
    for half in range(COLS // LANES):
        part = d_states.at[(index % 2) * (COLS // LANES) + half]
        part[...] = d_hidden[:, half * LANES : (half + 1) * LANES]
        lanes = slice(cols.start + half * LANES, cols.start + (half + 1) * LANES)
        far = slice(hidden + lanes.start, hidden + lanes.stop)
        backward_scan(linked, retain, states, slope, part, d_proj, lanes, far)


def backward_conv(d_proj, w_in, d_conv):
    for rows in blocks(d_proj.shape[0], 256):
        d_conv[rows] = dot_nt(d_proj[rows], w_in[...])


def backward_mix(linked, x, gain, taps, d_middle, d_conv, out):
    length, width = x.shape
    factor = exit_factor((GROUP, width), linked)
    for ahead in range(3):
        block = d_conv[ahead * GROUP : (ahead + 1) * GROUP]
        d_conv[length + ahead * GROUP : length + (ahead + 1) * GROUP] = pltpu.roll(block, GROUP - 1, 0) * factor
    gain_total = jnp.zeros((8, width), f32)
    tap_totals = [jnp.zeros((8, width), f32) for _ in range(4)]
    for rows in blocks(length, 128):
        values = x[rows].astype(f32)
        scale = inverse_norm(values)
        unit = values * scale
        normed = unit * gain
        d_normed = jnp.zeros_like(unit)
        for ahead in range(4):
            shifted = d_conv[rows.start + ahead * GROUP : rows.stop + ahead * GROUP]
            tap_totals[ahead] = tap_totals[ahead] + fold_rows(normed * shifted)
            d_normed = d_normed + shifted * taps[ahead]
        gain_total = gain_total + fold_rows(d_normed * unit)
        d_unit = d_normed * gain
        mean = jnp.mean(d_unit * unit, axis=-1, keepdims=True)
        out[rows] = (d_middle[rows] + scale * (d_unit - unit * mean)).astype(bf16)
    return gain_total, tap_totals


MESH = pl.DeviceIdType.MESH
GROUPS = 16
LIMIT = 63 * 2**20 + 2**19
DOWN, UP, OUT, IN = range(4)


class Place:
    def __init__(self, per_group):
        self.core = lax.axis_index("section")
        self.index = lax.axis_index("dp")
        self.per_group = per_group
        self.inner = lax.rem(self.index, per_group)
        group = lax.div(self.index, per_group)
        low = lax.rem(group, 2)
        high = lax.rem(lax.div(group, 2), 2)
        near = lax.rem(lax.div(group, 4), 2)
        far = lax.div(group, 8)
        first = low + self.core * (high - low)
        third = high + self.core * (low - high)
        self.digits = (first, near, third, far)

    def group(self, digits):
        first, near, third, far = digits
        low = first + self.core * (third - first)
        high = third + self.core * (first - third)
        return far * 8 + near * 4 + high * 2 + low

    def other_core(self):
        return (1 - self.core, self.index)

    def across(self, stage):
        digits = list(self.digits)
        digits[stage] = 1 - digits[stage]
        return (self.core, self.group(digits) * self.per_group + self.inner)

    def shards(self, stage, mine):
        chosen = self.digits[stage] if mine else 1 - self.digits[stage]
        found = [list(self.digits[:stage]) + [chosen]]
        for _ in range(stage + 1, 4):
            found = [digits + [value] for digits in found for value in range(2)]
        return [self.group(digits) for digits in found]


def remote(source, target, sems, device):
    return pltpu.make_async_remote_copy(
        src_ref=source, dst_ref=target, send_sem=sems.at[0], recv_sem=sems.at[1], device_id=device, device_id_type=MESH
    )


def send_stage(place, stage, own, landing, sems):
    for slot, group in enumerate(place.shards(stage, False)):
        remote(own.at[group], landing.at[slot], sems, place.across(stage)).start()


def take_stage(place, stage, own, landing, sems):
    remote(landing, landing, sems, place.across(stage)).wait()
    for slot, group in enumerate(place.shards(stage, True)):
        target = own.at[group]
        target[...] = target[...] + landing[slot]


def train_body(per_group, *refs):
    refs = list(refs)

    def take(count):
        taken = refs[:count]
        del refs[:count]
        return taken

    inputs, joined, cotangent, gain_a, taps, w_in, w_out, gain_b, w_up, w_down = take(10)
    layer_out, input_grads, g_in, g_out, g_up, g_down, small_out = take(7)
    far_weights = take(4)
    stored = take(9)
    xb, dy, stage_a, stage_b, turned, conv, retain, states, slope, middle, normed_low, act, act_slope, normed, update = take(15)
    weights = take(4)
    params, own_params, small, small_land = take(4)
    own = [take(4), take(4)]
    out_first, in_first = take(3), take(3)
    out_first.append(out_first[UP])
    in_first.append(in_first[UP])
    landing = [[take(4) for _ in range(4)], [take(4) for _ in range(3)]]
    landing[1].insert(0, landing[0][0])
    result = take(4)
    in_sems, weight_sems, store_sems, far_sems, param_sems, move_sems = take(6)
    first_sems, stage_sems, last_sems, small_sems, credits, stage_credits = take(6)
    assert not refs

    place = Place(per_group)
    core = place.core
    partner = place.other_core()
    linked = jnp.where(core == 0, joined[0, 0], joined[1, 0]).astype(f32)
    w_in_v, w_out_v, w_up_v, w_down_v = weights
    final = {DOWN: g_down, UP: g_up, OUT: g_out, IN: g_in}
    length, width = xb.shape

    barrier = pltpu.get_barrier_semaphore()
    greeted = [partner] + [place.across(stage) for stage in range(4)]
    for device in greeted:
        pl.semaphore_signal(barrier, inc=1, device_id=device, device_id_type=MESH)
    fetch_x = pltpu.make_async_copy(inputs.at[core, 0], stage_a, in_sems.at[0])
    fetch_x.start()
    fetch_dy = pltpu.make_async_copy(cotangent.at[core, 0], stage_b, in_sems.at[1])
    fetch_dy.start()
    own_params[...] = jnp.concatenate(
        [gain_a[...].astype(f32), taps[0].astype(f32), gain_b[...].astype(f32), jnp.zeros((2, width), f32)], axis=0
    )
    own_weights = [weight.at[0] for weight in (w_in, w_out, w_up, w_down)]

    def load(number, layer, arriving):
        @pl.when(core == layer)
        def _():
            pltpu.make_async_copy(own_weights[number], weights[number], weight_sems.at[number]).start()

        @pl.when(core != layer)
        def _():
            if arriving:
                remote(own_weights[number], far_weights[number], far_sems.at[number], partner).wait_recv()
            pltpu.make_async_copy(far_weights[number], weights[number], weight_sems.at[number]).start()

    def loaded(number):
        pltpu.make_async_copy(own_weights[number], weights[number], weight_sems.at[number]).wait()

    pl.semaphore_wait(barrier, len(greeted))
    to_params = remote(own_params, params.at[core], param_sems, partner)
    to_params.start()
    for number in range(4):
        remote(own_weights[number], far_weights[number], far_sems.at[number], partner).start()
    params[core] = own_params[...]

    def gain_a_of(layer):
        return params[layer, 0:1, :]

    def taps_of(layer):
        return [params[layer, 1 + tap : 2 + tap, :] for tap in range(4)]

    def gain_b_of(layer):
        return params[layer, 5:6, :]

    kept = (conv, retain, states, slope, middle, normed_low, act, act_slope, xb)

    def store(number):
        pltpu.make_async_copy(kept[number], stored[number], store_sems.at[number]).start()

    def stored_done(number):
        pltpu.make_async_copy(kept[number], stored[number], store_sems.at[number]).wait()

    def restore(number):
        pltpu.make_async_copy(stored[number], kept[number], store_sems.at[number]).start()

    def restored(number):
        pltpu.make_async_copy(stored[number], kept[number], store_sems.at[number]).wait()

    def publish(source, target, layer, number):
        @pl.when(core == layer)
        def _():
            pltpu.make_async_copy(source, target.at[0, core, 0], move_sems.at[number, 0]).start()

        @pl.when(core != layer)
        def _():
            remote(source, target.at[0, core, 0], move_sems.at[number], partner).start()

    def published(source, target, layer, number):
        @pl.when(core == layer)
        def _():
            pltpu.make_async_copy(source, target.at[0, core, 0], move_sems.at[number, 0]).wait()
            remote(source, target.at[0, 1 - core, 0], move_sems.at[number], partner).wait_recv()

        @pl.when(core != layer)
        def _():
            remote(source, target.at[0, core, 0], move_sems.at[number], partner).wait_send()

    fetch_x.wait()
    swap_order(stage_a, xb, update)
    store(8)
    to_params.wait()
    forward_mix(linked, xb, gain_a_of(0), taps_of(0), normed, conv)
    store(0)
    fetch_dy.wait()
    swap_order(stage_b, dy, update)
    chunks = states.shape[1] // COLS
    load(0, 0, True)
    loaded(0)
    for index in range(chunks):
        forward_gates(linked, conv, w_in_v, retain, update, states, act_slope, slope, index)
        if index == chunks // 2:
            load(1, 0, True)
    load(2, 0, True)
    load(0, 1, True)
    for number in (1, 2, 3):
        store(number)
    loaded(1)
    forward_middle(xb, act_slope, w_out_v, gain_b_of(0), middle, normed_low)
    load(3, 0, True)
    load(1, 1, True)
    store(4)
    store(5)
    loaded(2)
    forward_up(normed_low, w_up_v, act, act_slope)
    load(2, 1, True)
    store(6)
    store(7)
    stored_done(8)
    loaded(3)
    forward_down(middle, act, w_down_v, xb)
    load(3, 1, True)

    swap_order(xb, stage_a, update)
    publish(stage_a, layer_out, 0, 0)
    stored_done(0)
    forward_mix(linked, xb, gain_a_of(1), taps_of(1), normed, conv)
    for number in (1, 2, 3, 7):
        stored_done(number)
    loaded(0)
    for index in range(chunks):
        forward_gates(linked, conv, w_in_v, retain, update, states, act_slope, slope, index)
    stored_done(4)
    stored_done(5)
    loaded(1)
    forward_middle(xb, act_slope, w_out_v, gain_b_of(1), middle, normed_low)
    stored_done(6)
    loaded(2)
    forward_up(normed_low, w_up_v, act, act_slope)
    loaded(3)
    forward_down(middle, act, w_down_v, stage_b)
    swap_order(stage_b, stage_b, update)
    publish(stage_b, layer_out, 1, 1)

    def half_of(piece, which):
        size = own[0][piece].shape[2]
        return pl.ds(pl.multiple_of(which * size, size), size)

    def send_first(layer, piece):
        if layer == 0 or piece == IN:
            pl.semaphore_wait(credits.at[UP if piece == IN else piece], 1)
        remote(out_first[piece], in_first[piece], first_sems.at[piece], partner).start()

    def take_first(piece):
        remote(out_first[piece], in_first[piece], first_sems.at[piece], partner).wait()

    def free_first(layer, piece):
        if layer == 1 or piece == UP:
            pl.semaphore_signal(credits.at[UP if piece == IN else piece], inc=1, device_id=partner, device_id_type=MESH)

    def send(layer, piece, stage):
        if layer == 0 and stage == 0:
            pl.semaphore_wait(stage_credits.at[piece], 1)
        send_stage(place, stage, own[layer][piece], landing[layer][stage][piece], stage_sems.at[layer, piece, stage])

    def step(layer, piece, stage):
        own_piece, land = own[layer][piece], landing[layer][stage][piece]
        sems = stage_sems.at[layer, piece, stage]
        if stage < 3:
            take_stage(place, stage, own_piece, land, sems)
            if layer == 1 and stage == 0:
                pl.semaphore_signal(stage_credits.at[piece], inc=1, device_id=place.across(0), device_id_type=MESH)
            send(layer, piece, stage + 1)
            return
        remote(land, land, sems, place.across(3)).wait()
        total = own_piece[place.group(place.digits)].astype(f32) + land[0].astype(f32)
        near = half_of(piece, core)

        @pl.when(core == layer)
        def _():
            final[piece][0, :, near] = total

        @pl.when(core != layer)
        def _():
            result[piece][...] = total
            remote(result[piece], final[piece].at[0, :, near], last_sems.at[piece], partner).start()

    def grouped(values, piece):
        rows = own[0][piece].shape[1]
        return values.reshape(GROUPS, rows, values.shape[1])

    def backward(layer, plan):
        def run(point):
            for item in plan.get(point, ()):
                step(*item)

        near_down, far_down = half_of(DOWN, core), half_of(DOWN, 1 - core)
        if layer == 0:
            restored(5)
        turned[...] = normed_low[...].T
        if layer == 0:
            restored(6)
        inner = act.shape[1]
        rows_down = own[0][DOWN].shape[1]
        for cols in blocks(inner, COLS):
            groups = slice(cols.start // rows_down, cols.stop // rows_down)
            part = dot_tn(act[:, cols], dy[:, far_down]).astype(bf16)
            out_first[DOWN][groups] = part.reshape(COLS // rows_down, rows_down, part.shape[1])
        send_first(layer, DOWN)
        if layer == 0:
            restored(7)
            loaded(3)

        def d_pre_part(which, offset):
            start = which * (inner // 2) + offset
            cols = pl.ds(pl.multiple_of(start, COLS), COLS)
            d_act = dot_nt(dy[...], w_down_v[cols, :])
            values = (d_act * act_slope[:, cols].astype(f32)).astype(bf16)
            act_slope[:, cols] = values
            return dot(turned[...], values)

        for offset in range(0, inner // 2, COLS):
            part = d_pre_part(1 - core, offset)
            out_first[UP][:, :, offset : offset + COLS] = grouped(part.astype(bf16), UP)
        send_first(layer, UP)
        run("up sent")
        take_first(DOWN)
        for cols in blocks(inner, COLS):
            groups = slice(cols.start // rows_down, cols.stop // rows_down)
            part = dot_tn(act[:, cols], dy[:, near_down])
            part = part.reshape(COLS // rows_down, rows_down, part.shape[1])
            own[layer][DOWN][groups] = (part + in_first[DOWN][groups].astype(f32)).astype(bf16)
        free_first(layer, DOWN)
        if layer == 1:
            restore(6)
        send(layer, DOWN, 0)
        take_first(UP)
        for offset in range(0, inner // 2, COLS):
            part = grouped(d_pre_part(core, offset), UP)
            cols = slice(offset, offset + COLS)
            own[layer][UP][:, :, cols] = (part + in_first[UP][:, :, cols].astype(f32)).astype(bf16)
        free_first(layer, UP)
        if layer == 1:
            load(3, 0, False)
        send(layer, UP, 0)
        run("up done")
        if layer == 0:
            loaded(2)
            restored(4)
        mlp_total = backward_up(dy, act_slope, w_up_v, middle, gain_b_of(layer), middle, normed_low)
        if layer == 1:
            load(2, 0, False)
        run("middle")
        if layer == 0:
            restored(0)
            restored(2)
        turned[...] = conv[...].T
        if layer == 1:
            restore(0)
        near_out, far_out = half_of(OUT, core), half_of(OUT, 1 - core)
        rows_out = own[0][OUT].shape[1]
        hidden = states.shape[1]
        for cols in blocks(hidden, COLS):
            groups = slice(cols.start // rows_out, cols.stop // rows_out)
            part = dot_tn(states[:, cols].astype(bf16), normed_low[:, far_out]).astype(bf16)
            out_first[OUT][groups] = part.reshape(COLS // rows_out, rows_out, part.shape[1])
        send_first(layer, OUT)
        if layer == 0:
            restored(1)
            restored(3)
            loaded(1)
        for index in range(hidden // COLS):
            backward_gates(linked, normed_low, w_out_v, retain, states, slope, update, act_slope, index)
            if index == 1:
                run("gates")
        for offset in range(0, hidden, COLS):
            cols = pl.ds(pl.multiple_of((1 - core) * hidden + offset, COLS), COLS)
            part = dot(turned[...], act_slope[:, cols])
            out_first[IN][:, :, offset : offset + COLS] = grouped(part.astype(bf16), IN)
        send_first(layer, IN)
        take_first(OUT)
        for cols in blocks(hidden, COLS):
            groups = slice(cols.start // rows_out, cols.stop // rows_out)
            part = dot_tn(states[:, cols].astype(bf16), normed_low[:, near_out])
            part = part.reshape(COLS // rows_out, rows_out, part.shape[1])
            own[layer][OUT][groups] = (part + in_first[OUT][groups].astype(f32)).astype(bf16)
        send(layer, OUT, 0)
        free_first(layer, OUT)
        if layer == 1:
            for number in (1, 2, 3, 5):
                restore(number)
            load(1, 0, False)
        run("out done")
        if layer == 0:
            loaded(0)
        backward_conv(act_slope, w_in_v, normed)
        take_first(IN)
        for offset in range(0, hidden, COLS):
            source = pl.ds(pl.multiple_of(core * hidden + offset, COLS), COLS)
            part = grouped(dot(turned[...], act_slope[:, source]), IN)
            cols = slice(offset, offset + COLS)
            own[layer][IN][:, :, cols] = (part + in_first[IN][:, :, cols].astype(f32)).astype(bf16)
        send(layer, IN, 0)
        free_first(layer, IN)
        if layer == 1:
            restore(7)
            load(0, 0, False)
        run("in done")
        if layer == 0:
            restored(8)
        mix_total, tap_totals = backward_mix(linked, xb, gain_a_of(layer), taps_of(layer), middle, normed, dy)
        if layer == 1:
            restore(4)
            restore(8)
        totals = [mix_total] + tap_totals + [mlp_total]
        small[layer] = jnp.concatenate(
            [jnp.sum(total, axis=0, keepdims=True) for total in totals] + [jnp.zeros((2, width), f32)], axis=0
        )

    backward(
        1,
        {
            "gates": [(1, DOWN, 0)],
            "out done": [(1, UP, 0)],
            "in done": [(1, DOWN, 1)],
        },
    )
    published(stage_a, layer_out, 0, 0)
    swap_order(dy, stage_a, update)
    publish(stage_a, input_grads, 1, 2)
    step(1, OUT, 0)
    backward(
        0,
        {
            "up sent": [(1, UP, 1), (1, DOWN, 2)],
            "up done": [(1, IN, 0), (1, OUT, 1), (1, UP, 2)],
            "middle": [(1, DOWN, 3), (1, OUT, 2)],
            "gates": [(1, UP, 3)],
            "out done": [(1, IN, 1), (0, DOWN, 0), (1, OUT, 3)],
            "in done": [(1, IN, 2), (0, UP, 0)],
        },
    )
    devices = [partner] + [place.across(stage) for stage in range(4)]

    def small_start(number):
        remote(small, small_land.at[number], small_sems.at[number], devices[number]).start()

    def small_take(number):
        remote(small, small_land.at[number], small_sems.at[number], devices[number]).wait()
        small[...] = small[...] + small_land[number]

    small_start(0)
    published(stage_b, layer_out, 1, 1)
    swap_order(dy, stage_b, update)
    publish(stage_b, input_grads, 0, 3)
    small_take(0)
    small_start(1)
    for item in [(0, DOWN, 1), (1, IN, 3), (0, OUT, 0)]:
        step(*item)
    small_take(1)
    small_start(2)
    for item in [(0, UP, 1), (0, DOWN, 2), (0, IN, 0), (0, OUT, 1)]:
        step(*item)
    small_take(2)
    small_start(3)
    for item in [(0, UP, 2), (0, DOWN, 3), (0, IN, 1), (0, OUT, 2)]:
        step(*item)
    small_take(3)
    small_start(4)
    for item in [(0, UP, 3), (0, IN, 2), (0, OUT, 3)]:
        step(*item)
    small_take(4)
    small_out[...] = small[core]
    step(0, IN, 3)

    published(stage_a, input_grads, 1, 2)
    published(stage_b, input_grads, 0, 3)
    for number in range(4):
        remote(own_weights[number], far_weights[number], far_sems.at[number], partner).wait_send()
    for layer in range(2):
        for piece in range(4):
            far = half_of(piece, 1 - core)

            @pl.when(core == layer)
            def _():
                remote(result[piece], final[piece].at[0, :, far], last_sems.at[piece], partner).wait_recv()

            @pl.when(core != layer)
            def _():
                remote(result[piece], final[piece].at[0, :, far], last_sems.at[piece], partner).wait_send()


def train(per_group, inputs, joined, cotangent, gain_a, taps, w_in, w_out, gain_b, w_up, w_down):
    length, width = inputs.shape[2:]
    hidden, inner = w_out.shape[1], w_up.shape[2]
    batches = inputs.shape[0]
    shape = jax.ShapeDtypeStruct
    vmem, anywhere = pl.BlockSpec(memory_space=pltpu.VMEM), pl.BlockSpec(memory_space=pl.ANY)
    smem = pl.BlockSpec(memory_space=pltpu.SMEM)
    weights = (w_in, w_out, w_up, w_down)
    pieces = [(weight.shape[1] // GROUPS, weight.shape[2]) for weight in (w_down, w_up, w_out, w_in)]
    kept = [
        ((length, width), bf16),
        ((length, hidden), f32),
        ((length, hidden), f32),
        ((length, hidden), bf16),
        ((length, width), f32),
        ((length, width), bf16),
        ((length, inner), bf16),
        ((length, inner), bf16),
        ((length, width), bf16),
    ]
    outs = [shape((1, batches, 1, length, width), bf16)] * 2
    outs += [shape((1,) + pieces[piece], f32) for piece in (IN, OUT, UP, DOWN)]
    outs += [shape((8, width), f32)]
    spaces = [anywhere] * 2 + [vmem] * 5
    outs += [shape(weight.shape[1:], bf16) for weight in weights]
    outs += [shape(*entry) for entry in kept]
    spaces += [anywhere] * (len(outs) - len(spaces))

    def halves(count, kind):
        lead = (count,) if count else ()
        return [pltpu.VMEM(lead + (rows, columns // 2), kind) for rows, columns in pieces]

    small_rows = pltpu.VMEM((8, width), f32)
    dma = pltpu.SemaphoreType.DMA
    scratch = [pltpu.VMEM((length, width), bf16) for _ in range(4)]
    scratch += [pltpu.VMEM((width, length), bf16)]
    scratch += [pltpu.VMEM(*entry) for entry in kept[:8]]
    scratch += [pltpu.VMEM((length + 3 * GROUP, width), f32), pltpu.VMEM((2 * COLS // LANES, length, LANES), f32)]
    scratch += [pltpu.VMEM(weight.shape[1:], bf16) for weight in weights]
    scratch += [pltpu.VMEM((2, 8, width), f32), small_rows, pltpu.VMEM((2, 8, width), f32), pltpu.VMEM((5, 2, 8, width), f32)]
    scratch += halves(GROUPS, bf16) * 2 + halves(GROUPS, bf16)[:3] * 2
    for layer in range(2):
        for stage in range(layer, 4):
            scratch += halves(GROUPS >> (stage + 1), bf16)
    scratch += halves(0, f32)
    scratch += [dma((2,)), dma((4,)), dma((len(kept),)), dma((4, 2)), dma((2,)), dma((4, 2))]
    scratch += [dma((4, 2)), dma((2, 4, 4, 2)), dma((4, 2)), dma((5, 2))]
    scratch += [pltpu.SemaphoreType.REGULAR((3,)), pltpu.SemaphoreType.REGULAR((4,))]
    results = pl.pallas_call(
        lambda *refs: train_body(per_group, *refs),
        out_shape=outs,
        in_specs=[anywhere, smem, anywhere, vmem, vmem, anywhere, anywhere, vmem, anywhere, anywhere],
        out_specs=spaces,
        scratch_shapes=scratch,
        compiler_params=pltpu.CompilerParams(vmem_limit_bytes=LIMIT, collective_id=0, has_side_effects=True),
        name="train",
    )(inputs, joined, cotangent, gain_a, taps, w_in, w_out, gain_b, w_up, w_down)
    return results[:7]


def local(inputs, joined, cotangent, gain_mix, conv_taps, w_in, w_out, gain_mlp, w_up, w_down):
    dp = lax.axis_size("dp")
    per_group = dp // GROUPS
    layer_out, input_grads, g_in, g_out, g_up, g_down, small = train(
        per_group, inputs, joined, cotangent, gain_mix, conv_taps, w_in, w_out, gain_mlp, w_up, w_down
    )
    if per_group > 1:
        members = [[group * per_group + inner for inner in range(per_group)] for group in range(GROUPS)]

        def finish(grad):
            return lax.psum_scatter(grad, "dp", scatter_dimension=1, axis_index_groups=members, tiled=True)

        g_in, g_out, g_up, g_down = [finish(grad) for grad in (g_in, g_out, g_up, g_down)]
        small = lax.psum(small, "dp", axis_index_groups=members)
    lanes = small.shape[1] // dp
    small = lax.dynamic_slice_in_dim(small, lax.axis_index("dp") * lanes, lanes, 1)
    return (layer_out, input_grads, small[0:1], small[None, 1:5], g_in, g_out, small[5:6], g_up, g_down)


def solution(mesh):
    placed = (
        P(None, "dp", None, None),
        P(None, "dp"),
        P(None, "dp", None, None),
        P("section", None),
        P("section", None, None),
        P("section", None, None),
        P("section", None, None),
        P("section", None),
        P("section", None, None),
        P("section", None, None),
    )
    return jax.shard_map(
        local,
        mesh=mesh,
        in_specs=placed,
        out_specs=(
            P("section", None, "dp", None, None),
            P("section", None, "dp", None, None),
            P("section", "dp"),
            P("section", None, "dp"),
            P("section", "dp", None),
            P("section", "dp", None),
            P("section", "dp"),
            P("section", "dp", None),
            P("section", "dp", None),
        ),
        check_vma=False,
    )
```

```python
import jax
import jax.numpy as jnp
from jax import lax
from jax.experimental import pallas as pl
from jax.experimental.pallas import tpu as pltpu
from jax.sharding import PartitionSpec as P

f32 = jnp.float32
bf16 = jnp.bfloat16
epsilon = 1e-06
GROUP = 32
COLS = 256
LANES = 128
GELU_A = 0.7978845608028654
GELU_B = GELU_A * 0.044715


def dot(left, right):
    return jnp.dot(left, right, preferred_element_type=f32)


def dot_nt(left, right):
    return lax.dot_general(left, right, (((1,), (1,)), ((), ())), preferred_element_type=f32)


def dot_tn(left, right):
    return lax.dot_general(left, right, (((0,), (0,)), ((), ())), preferred_element_type=f32)


def segment_rows(shape):
    return lax.broadcasted_iota(jnp.int32, shape, 0)


def entry_factor(shape, linked):
    row = segment_rows(shape)
    return jnp.where(row == 0, 0.0, jnp.where(row == GROUP // 2, linked, 1.0))


def exit_factor(shape, linked):
    row = segment_rows(shape)
    return jnp.where(row == GROUP - 1, 0.0, jnp.where(row == GROUP // 2 - 1, linked, 1.0))


def blocks(total, size):
    return [slice(start, start + size) for start in range(0, total, size)]


def inverse_norm(values):
    return lax.rsqrt(jnp.mean(values * values, axis=-1, keepdims=True) + epsilon)


def fold_rows(values):
    rows, width = values.shape
    return jnp.sum(values.reshape(rows // 8, 8, width), axis=0)


def logistic_pair(logit):
    away = jnp.exp(-jnp.maximum(logit, -80.0))
    opened = 1.0 / (1.0 + away)
    return opened, away * opened


def softplus_parts(value):
    small = jnp.exp(-jnp.abs(value))
    whole = 1.0 + small
    inverse = pltpu.reciprocal(whole, approx=True)
    log_part = jnp.where(small < 2.0**-10, small * (1.0 - 0.5 * small), jnp.log(whole))
    slope = jnp.where(value >= 0, inverse, small * inverse)
    return jnp.maximum(value, 0.0) + log_part, slope


def gelu_half(value, square):
    return 0.5 + 0.5 * jnp.tanh(value * (GELU_A + GELU_B * square))


def gelu(value):
    return value * gelu_half(value, value * value)


def gelu_slope(value):
    square = value * value
    half = gelu_half(value, square)
    return half * (1.0 + (1.0 - half) * (value * (2.0 * GELU_A + 6.0 * GELU_B * square)))


def swap_order(source, target):
    length, width = source.shape
    steps = length // GROUP
    assert steps == GROUP
    target[...] = jnp.swapaxes(source[...].reshape(steps, GROUP, width), 0, 1).reshape(length, width)


def forward_mix(linked, x, gain, taps, normed, conv):
    length, width = x.shape
    lead = 3 * GROUP
    for rows in blocks(length, 128):
        values = x[rows].astype(f32)
        normed[lead + rows.start : lead + rows.stop] = values * inverse_norm(values) * gain
    factor = entry_factor((GROUP, width), linked)
    for back in range(1, 4):
        start = lead + length - back * GROUP
        block = normed[start : start + GROUP]
        normed[lead - back * GROUP : lead - (back - 1) * GROUP] = pltpu.roll(block, 1, 0) * factor
    for rows in blocks(length, 128):
        total = normed[lead + rows.start : lead + rows.stop] * taps[0]
        for back in range(1, 4):
            start = lead - back * GROUP + rows.start
            total = total + normed[start : start + 128] * taps[back]
        conv[rows] = total.astype(bf16)


def forward_scan(linked, retain, update, states, states_low, cols):
    length = retain.shape[0]
    steps = length // GROUP
    shape = (GROUP, LANES)
    ends = update[0:GROUP]
    spans = retain[0:GROUP, cols]
    for step in range(1, steps):
        rows = slice(step * GROUP, (step + 1) * GROUP)
        keep = retain[rows, cols]
        ends = keep * ends + update[rows]
        spans = keep * spans
    factor = entry_factor(shape, linked)
    spans = spans * factor
    row = segment_rows(shape)
    distance = 1
    while distance < GROUP:
        reach = jnp.where(row >= distance, spans, 0.0)
        ends = ends + reach * pltpu.roll(ends, distance, 0)
        spans = reach * pltpu.roll(spans, distance, 0)
        distance = 2 * distance
    carry = pltpu.roll(ends, 1, 0) * factor
    for step in range(steps):
        rows = slice(step * GROUP, (step + 1) * GROUP)
        carry = retain[rows, cols] * carry + update[rows]
        states[rows, cols] = carry
        states_low[rows, cols] = carry.astype(bf16)


def forward_gates(linked, conv, w_in, retain, update, states, states_low, slope, index):
    hidden = states.shape[1]
    cols = slice(index * COLS, (index + 1) * COLS)
    far = slice(hidden + index * COLS, hidden + (index + 1) * COLS)
    opened, kept = logistic_pair(dot(conv[...], w_in[:, cols]))
    retain[:, cols] = kept
    soft, soft_slope = softplus_parts(dot(conv[...], w_in[:, far]))
    slope[:, cols] = (opened * soft_slope).astype(bf16)
    added = opened * soft
    for half in range(COLS // LANES):
        part = update.at[(index % 2) * (COLS // LANES) + half]
        part[...] = added[:, half * LANES : (half + 1) * LANES]
        lanes = slice(cols.start + half * LANES, cols.start + (half + 1) * LANES)
        forward_scan(linked, retain, part, states, states_low, lanes)


def forward_middle(x, states_low, w_out, gain, middle, normed_low):
    hidden = w_out.shape[0]
    for rows in blocks(x.shape[0], 256):
        values = x[rows].astype(f32) + dot(states_low[rows, 0:hidden], w_out[...])
        middle[rows] = values
        normed_low[rows] = (values * inverse_norm(values) * gain).astype(bf16)


def forward_up(normed_low, w_up, act, pre_act):
    for cols in blocks(act.shape[1], COLS):
        values = dot(normed_low[...], w_up[:, cols])
        act[:, cols] = gelu(values).astype(bf16)
        pre_act[:, cols] = values.astype(bf16)


def forward_down(middle, act, w_down, out):
    for rows in blocks(middle.shape[0], 256):
        out[rows] = (middle[rows] + dot(act[rows], w_down[...])).astype(bf16)


def backward_up(dy, d_pre, w_up, middle, gain, d_middle, d_middle_low):
    total = jnp.zeros((8, dy.shape[1]), f32)
    for rows in blocks(dy.shape[0], 256):
        d_normed = dot_nt(d_pre[rows], w_up[...])
        values = middle[rows]
        scale = inverse_norm(values)
        unit = values * scale
        total = total + fold_rows(d_normed * unit)
        d_unit = d_normed * gain
        mean = jnp.mean(d_unit * unit, axis=-1, keepdims=True)
        result = dy[rows].astype(f32) + scale * (d_unit - unit * mean)
        d_middle[rows] = result
        d_middle_low[rows] = result.astype(bf16)
    return total


def backward_scan(linked, retain, states, slope, d_states, d_proj, cols, far):
    length = retain.shape[0]
    steps = length // GROUP
    shape = (GROUP, LANES)
    last = slice(length - GROUP, length)
    running = d_states[last]
    spans = retain[last, cols]
    for step in range(steps - 2, -1, -1):
        rows = slice(step * GROUP, (step + 1) * GROUP)
        after = retain[(step + 1) * GROUP : (step + 2) * GROUP, cols]
        running = d_states[rows] + after * running
        spans = spans * retain[rows, cols]
    entry = entry_factor(shape, linked)
    ends = retain[0:GROUP, cols] * running * entry
    spans = spans * entry
    row = segment_rows(shape)
    distance = 1
    while distance < GROUP:
        reach = jnp.where(row < GROUP - distance, spans, 0.0)
        ends = ends + reach * pltpu.roll(ends, GROUP - distance, 0)
        spans = reach * pltpu.roll(spans, GROUP - distance, 0)
        distance = 2 * distance
    running = jnp.where(row < GROUP - 1, pltpu.roll(ends, GROUP - 1, 0), 0.0)
    first_before = pltpu.roll(states[last, cols], 1, 0) * entry
    for step in range(steps - 1, -1, -1):
        rows = slice(step * GROUP, (step + 1) * GROUP)
        running = d_states[rows] + running
        keep = retain[rows, cols]
        before = states[(step - 1) * GROUP : step * GROUP, cols] if step else first_before
        decayed = keep * running
        d_proj[rows, cols] = (decayed * (states[rows, cols] - before)).astype(bf16)
        d_proj[rows, far] = (running * slope[rows, cols].astype(f32)).astype(bf16)
        running = decayed


def backward_gates(linked, d_middle_low, w_out, retain, states, slope, d_states, d_proj, index):
    hidden = states.shape[1]
    cols = slice(index * COLS, (index + 1) * COLS)
    d_hidden = dot_nt(d_middle_low[...], w_out[cols])
    for half in range(COLS // LANES):
        part = d_states.at[(index % 2) * (COLS // LANES) + half]
        part[...] = d_hidden[:, half * LANES : (half + 1) * LANES]
        lanes = slice(cols.start + half * LANES, cols.start + (half + 1) * LANES)
        far = slice(hidden + lanes.start, hidden + lanes.stop)
        backward_scan(linked, retain, states, slope, part, d_proj, lanes, far)


def backward_conv(d_proj, w_in, d_conv):
    for rows in blocks(d_proj.shape[0], 256):
        d_conv[rows] = dot_nt(d_proj[rows], w_in[...])


def backward_mix(linked, x, gain, taps, d_middle, d_conv, out):
    length, width = x.shape
    factor = exit_factor((GROUP, width), linked)
    for ahead in range(3):
        block = d_conv[ahead * GROUP : (ahead + 1) * GROUP]
        d_conv[length + ahead * GROUP : length + (ahead + 1) * GROUP] = pltpu.roll(block, GROUP - 1, 0) * factor
    gain_total = jnp.zeros((8, width), f32)
    tap_totals = [jnp.zeros((8, width), f32) for _ in range(4)]
    for rows in blocks(length, 128):
        values = x[rows].astype(f32)
        scale = inverse_norm(values)
        unit = values * scale
        normed = unit * gain
        d_normed = jnp.zeros_like(unit)
        for ahead in range(4):
            shifted = d_conv[rows.start + ahead * GROUP : rows.stop + ahead * GROUP]
            tap_totals[ahead] = tap_totals[ahead] + fold_rows(normed * shifted)
            d_normed = d_normed + shifted * taps[ahead]
        gain_total = gain_total + fold_rows(d_normed * unit)
        d_unit = d_normed * gain
        mean = jnp.mean(d_unit * unit, axis=-1, keepdims=True)
        out[rows] = (d_middle[rows] + scale * (d_unit - unit * mean)).astype(bf16)
    return gain_total, tap_totals


MESH = pl.DeviceIdType.MESH
GROUPS = 16
LIMIT = 63 * 2**20 + 2**19
DOWN, UP, OUT, IN = range(4)
UNITS = ((DOWN, None), (UP, None), (OUT, None), (IN, 0), (IN, 1), (IN, 2), (IN, 3))


class Place:
    def __init__(self, per_group):
        self.core = lax.axis_index("section")
        self.index = lax.axis_index("dp")
        self.per_group = per_group
        self.inner = lax.rem(self.index, per_group)
        group = lax.div(self.index, per_group)
        low = lax.rem(group, 2)
        high = lax.rem(lax.div(group, 2), 2)
        near = lax.rem(lax.div(group, 4), 2)
        far = lax.div(group, 8)
        first = low + self.core * (high - low)
        third = high + self.core * (low - high)
        self.digits = (first, near, third, far)

    def group(self, digits):
        first, near, third, far = digits
        low = first + self.core * (third - first)
        high = third + self.core * (first - third)
        return far * 8 + near * 4 + high * 2 + low

    def other_core(self):
        return (1 - self.core, self.index)

    def across(self, stage):
        digits = list(self.digits)
        digits[stage] = 1 - digits[stage]
        return (self.core, self.group(digits) * self.per_group + self.inner)

    def position(self, group):
        low, high, near, far = group % 2, group // 2 % 2, group // 4 % 2, group // 8
        on_first = low * 8 + near * 4 + high * 2 + far
        on_second = high * 8 + near * 4 + low * 2 + far
        return on_first + self.core * (on_second - on_first)

    def range_of(self, stage, mine):
        start = sum(self.digits[before] * (8 >> before) for before in range(stage))
        digit = self.digits[stage]
        start = start + (digit if mine else 1 - digit) * (8 >> stage)
        return pl.ds(start, 8 >> stage)


def remote(source, target, sems, device):
    return pltpu.make_async_remote_copy(
        src_ref=source, dst_ref=target, send_sem=sems.at[0], recv_sem=sems.at[1], device_id=device, device_id_type=MESH
    )


def train_body(per_group, *refs):
    refs = list(refs)

    def take(count):
        taken = refs[:count]
        del refs[:count]
        return taken

    inputs, joined, cotangent, gain_a, taps, w_in, w_out, gain_b, w_up, w_down = take(10)
    layer_out, input_grads, g_in, g_out, g_up, g_down, small_out = take(7)
    far_weights = take(4)
    stored = take(9)
    xb, dy, stage_a, stage_b, turned, conv, retain, states, slope, middle, normed_low, act, pre_act, normed, update = take(15)
    weights = take(4)
    params, own_params, small, small_land = take(4)
    units = len(UNITS)
    own = [take(units), take(units)]
    out_first, in_first = take(3), take(3)
    landing = [[take(units) for _ in range(4)], [take(units) for _ in range(3)]]
    landing[1].insert(0, landing[0][0])
    result = take(units)
    in_sems, weight_sems, chunk_sems, spill_sems, store_sems, far_sems, param_sems, move_sems = take(8)
    first_sems, stage_sems, last_sems, small_sems, credits, stage_credits = take(6)
    assert not refs

    place = Place(per_group)
    core = place.core
    partner = place.other_core()
    linked = jnp.where(core == 0, joined[0:1, 0:1], joined[1:2, 0:1]).astype(f32)
    w_in_v, w_out_v, w_up_v, w_down_v = weights
    final = {DOWN: g_down, UP: g_up, OUT: g_out, IN: g_in}
    length, width = xb.shape
    hidden, inner = states.shape[1], act.shape[1]
    chunks = hidden // COLS

    barrier = pltpu.get_barrier_semaphore()
    greeted = [partner] + [place.across(stage) for stage in range(4)]
    for device in greeted:
        pl.semaphore_signal(barrier, inc=1, device_id=device, device_id_type=MESH)
    fetch_x = pltpu.make_async_copy(inputs.at[core, 0], stage_a, in_sems.at[0])
    fetch_x.start()
    fetch_dy = pltpu.make_async_copy(cotangent.at[core, 0], stage_b, in_sems.at[1])
    fetch_dy.start()
    own_params[...] = jnp.concatenate(
        [gain_a[...].astype(f32), taps[0].astype(f32), gain_b[...].astype(f32), jnp.zeros((2, width), f32)], axis=0
    )
    own_weights = [weight.at[0] for weight in (w_in, w_out, w_up, w_down)]

    def in_chunk(index):
        return [slice(side * hidden + index * COLS, side * hidden + (index + 1) * COLS) for side in range(2)]

    def load(number, layer):
        @pl.when(core == layer)
        def _():
            pltpu.make_async_copy(own_weights[number], weights[number], weight_sems.at[number]).start()

        @pl.when(core != layer)
        def _():
            pltpu.make_async_copy(far_weights[number], weights[number], weight_sems.at[number]).start()

    def loaded(number):
        pltpu.make_async_copy(own_weights[number], weights[number], weight_sems.at[number]).wait()

    def spill(number):
        @pl.when(core == 1)
        def _():
            pltpu.make_async_copy(weights[number], far_weights[number], spill_sems.at[number]).start()

    def load_second(number):
        @pl.when(core == 1)
        def _():
            pltpu.make_async_copy(weights[number], far_weights[number], spill_sems.at[number]).wait()

        @pl.when(core == 0)
        def _():
            if number:
                remote(own_weights[number], far_weights[number], far_sems.at[number], partner).wait_recv()
            else:
                for index in range(chunks):
                    both = pl.ds(index * 2 * COLS, 2 * COLS)
                    remote(own_weights[0].at[:, both], far_weights[0].at[:, both], chunk_sems.at[index], partner).wait_recv()

        load(number, 1)

    pl.semaphore_wait(barrier, len(greeted))
    to_params = remote(own_params, params.at[core], param_sems, partner)
    to_params.start()

    @pl.when(core == 0)
    def _():
        for index in range(chunks):
            for cols in in_chunk(index):
                pltpu.make_async_copy(own_weights[0].at[:, cols], w_in_v.at[:, cols], weight_sems.at[4 + index]).start()
        for index in range(chunks):
            for cols in in_chunk(index):
                remote(own_weights[0].at[:, cols], w_in_v.at[:, cols], chunk_sems.at[index], partner).start()
        for number in range(1, 4):
            pltpu.make_async_copy(own_weights[number], weights[number], weight_sems.at[number]).start()
            remote(own_weights[number], weights[number], far_sems.at[number], partner).start()

    @pl.when(core == 1)
    def _():
        for index in range(chunks):
            for cols in in_chunk(index):
                remote(own_weights[0].at[:, cols], far_weights[0].at[:, cols], chunk_sems.at[index], partner).start()
        for number in range(1, 4):
            remote(own_weights[number], far_weights[number], far_sems.at[number], partner).start()

    def loaded_first(number):
        @pl.when(core == 0)
        def _():
            loaded(number)

        @pl.when(core == 1)
        def _():
            remote(own_weights[number], weights[number], far_sems.at[number], partner).wait_recv()

        spill(number)

    def loaded_chunk(index):
        both = pl.ds(index * 2 * COLS, 2 * COLS)

        @pl.when(core == 0)
        def _():
            pltpu.make_async_copy(own_weights[0].at[:, both], w_in_v.at[:, both], weight_sems.at[4 + index]).wait()

        @pl.when(core == 1)
        def _():
            remote(own_weights[0].at[:, both], w_in_v.at[:, both], chunk_sems.at[index], partner).wait_recv()

    params[core] = own_params[...]

    def gain_a_of(layer):
        return params[layer, 0:1, :]

    def taps_of(layer):
        return [params[layer, 1 + tap : 2 + tap, :] for tap in range(4)]

    def gain_b_of(layer):
        return params[layer, 5:6, :]

    kept = (conv, retain, states, slope, middle, normed_low, act, pre_act, xb)

    def store(number):
        pltpu.make_async_copy(kept[number], stored[number], store_sems.at[number]).start()

    def stored_done(number):
        pltpu.make_async_copy(kept[number], stored[number], store_sems.at[number]).wait()

    def restore(number):
        pltpu.make_async_copy(stored[number], kept[number], store_sems.at[number]).start()

    def restored(number):
        pltpu.make_async_copy(stored[number], kept[number], store_sems.at[number]).wait()

    def publish(source, target, layer, number):
        @pl.when(core == layer)
        def _():
            pltpu.make_async_copy(source, target.at[0, core, 0], move_sems.at[number, 0]).start()

        @pl.when(core != layer)
        def _():
            remote(source, target.at[0, core, 0], move_sems.at[number], partner).start()

    def published(source, target, layer, number):
        @pl.when(core == layer)
        def _():
            pltpu.make_async_copy(source, target.at[0, core, 0], move_sems.at[number, 0]).wait()
            remote(source, target.at[0, 1 - core, 0], move_sems.at[number], partner).wait_recv()

        @pl.when(core != layer)
        def _():
            remote(source, target.at[0, core, 0], move_sems.at[number], partner).wait_send()

    fetch_x.wait()
    swap_order(stage_a, xb)
    store(8)
    to_params.wait()
    forward_mix(linked, xb, gain_a_of(0), taps_of(0), normed, conv)
    store(0)
    for index in range(chunks):
        loaded_chunk(index)
        forward_gates(linked, conv, w_in_v, retain, update, states, pre_act, slope, index)
    spill(0)
    for number in (1, 2, 3):
        store(number)
    loaded_first(1)
    forward_middle(xb, pre_act, w_out_v, gain_b_of(0), middle, normed_low)
    store(4)
    store(5)
    load_second(0)
    loaded_first(2)
    forward_up(normed_low, w_up_v, act, pre_act)
    load_second(1)
    store(6)
    store(7)
    stored_done(8)
    loaded_first(3)
    forward_down(middle, act, w_down_v, xb)
    load_second(2)

    swap_order(xb, stage_a)
    publish(stage_a, layer_out, 0, 0)
    stored_done(0)
    forward_mix(linked, xb, gain_a_of(1), taps_of(1), normed, conv)
    load_second(3)
    for number in (1, 2, 3, 7):
        stored_done(number)
    loaded(0)
    for index in range(chunks):
        forward_gates(linked, conv, w_in_v, retain, update, states, pre_act, slope, index)
    fetch_dy.wait()
    swap_order(stage_b, dy)
    stored_done(4)
    stored_done(5)
    loaded(1)
    forward_middle(xb, pre_act, w_out_v, gain_b_of(1), middle, normed_low)
    stored_done(6)
    loaded(2)
    loaded(3)

    def half_of(piece, which):
        size = 2 * width // 4 if piece in (DOWN, OUT) else inner // 2
        return pl.ds(pl.multiple_of(which * size, size), size)

    def within(piece, chunk):
        return slice(None) if chunk is None else slice(chunk * COLS, (chunk + 1) * COLS)

    def first_refs(unit):
        piece, chunk = UNITS[unit]
        place_of = UP if piece == IN else piece
        cols = within(piece, chunk)
        return out_first[place_of].at[:, :, cols], in_first[place_of].at[:, :, cols]

    def send_first(layer, unit):
        piece, chunk = UNITS[unit]
        if (layer == 0 and piece != IN) or chunk == 0:
            pl.semaphore_wait(credits.at[UP if piece == IN else piece], 1)
        remote(*first_refs(unit), first_sems.at[unit], partner).start()

    def take_first(unit):
        remote(*first_refs(unit), first_sems.at[unit], partner).wait()

    def free_first(layer, unit):
        piece, chunk = UNITS[unit]
        if piece == UP or (layer == 1 and chunk in (None, chunks - 1)):
            pl.semaphore_signal(credits.at[UP if piece == IN else piece], inc=1, device_id=partner, device_id_type=MESH)

    def send(layer, unit, stage):
        if layer == 0 and stage == 0:
            pl.semaphore_wait(stage_credits.at[unit], 1)
        source = own[layer][unit].at[place.range_of(stage, False)]
        remote(source, landing[layer][stage][unit], stage_sems.at[layer, unit, stage], place.across(stage)).start()

    def step(layer, unit, stage):
        mine, land = own[layer][unit].at[place.range_of(stage, True)], landing[layer][stage][unit]
        remote(mine, land, stage_sems.at[layer, unit, stage], place.across(stage)).wait()
        if stage < 3:
            mine[...] = mine[...] + land[...]
            if layer == 1 and stage == 0:
                pl.semaphore_signal(stage_credits.at[unit], inc=1, device_id=place.across(0), device_id_type=MESH)
            send(layer, unit, stage + 1)
            return
        total = mine[0].astype(f32) + land[0].astype(f32)
        target = final_part(unit, core)

        @pl.when(core == layer)
        def _():
            target[...] = total

        @pl.when(core != layer)
        def _():
            result[unit][...] = total
            remote(result[unit], target, last_sems.at[unit], partner).start()

    def final_part(unit, which):
        piece, chunk = UNITS[unit]
        if chunk is None:
            return final[piece].at[0, :, half_of(piece, which)]
        return final[piece].at[0, :, pl.ds(pl.multiple_of(which * hidden + chunk * COLS, COLS), COLS)]

    def own_put(layer, unit, first_group, values, cols=slice(None)):
        rows = own[layer][unit].shape[1]
        landed = first_refs(unit)[1]
        for number in range(values.shape[0] // rows):
            group = first_group + number
            total = values[number * rows : (number + 1) * rows] + landed[group, :, cols].astype(f32)
            own[layer][unit][place.position(group), :, cols] = total.astype(bf16)

    def out_put(unit, first_group, values, cols=slice(None)):
        target = first_refs(unit)[0]
        rows = target.shape[1]
        count = values.shape[0] // rows
        target[first_group : first_group + count, :, cols] = values.astype(bf16).reshape(count, rows, values.shape[1])

    def backward(layer, plan):
        def run(point):
            for unit, stage in plan.get(point, ()):
                if unit < 0:
                    step(1, -unit - 1, stage)
                else:
                    step(layer, unit, stage)

        def down_part(cols, which):
            return dot_tn(act[:, cols], dy[:, half_of(DOWN, which)])

        def d_pre_part(which, offset):
            start = which * (inner // 2) + offset
            cols = pl.ds(pl.multiple_of(start, COLS), COLS)
            d_act = dot_nt(dy[...], w_down_v[cols, :])
            values = (d_act * gelu_slope(pre_act[:, cols].astype(f32))).astype(bf16)
            pre_act[:, cols] = values
            return dot(turned[...], values)

        def out_part(cols, which):
            return dot_tn(states[:, cols].astype(bf16), normed_low[:, half_of(OUT, which)])

        def in_part(index, which):
            cols = pl.ds(pl.multiple_of(which * hidden + index * COLS, COLS), COLS)
            return dot(turned[...], pre_act[:, cols])

        rows_down = own[0][DOWN].shape[1]
        if layer == 1:
            forward_up(normed_low, w_up_v, act, pre_act)
        else:
            restored(6)
            restored(5)
        for cols in blocks(inner, COLS):
            out_put(DOWN, cols.start // rows_down, down_part(cols, 1 - core))
        turned[...] = normed_low[...].T
        send_first(layer, DOWN)
        run("down sent")
        if layer == 0:
            restored(7)
            loaded(3)
        for offset in range(0, inner // 2, COLS):
            out_put(UP, 0, d_pre_part(1 - core, offset), slice(offset, offset + COLS))
        if layer == 1:
            forward_down(middle, act, w_down_v, stage_b)
        send_first(layer, UP)
        run("up sent")
        take_first(DOWN)
        for cols in blocks(inner, COLS):
            own_put(layer, DOWN, cols.start // rows_down, down_part(cols, core))
        if layer == 1:
            swap_order(stage_b, stage_b)
            publish(stage_b, layer_out, 1, 1)
            restore(6)
        free_first(layer, DOWN)
        send(layer, DOWN, 0)
        run("down done")
        take_first(UP)
        for offset in range(0, inner // 2, COLS):
            own_put(layer, UP, 0, d_pre_part(core, offset), slice(offset, offset + COLS))
        free_first(layer, UP)
        send(layer, UP, 0)
        if layer == 1:
            load(3, 0)
        run("up done")
        if layer == 0:
            loaded(2)
            restored(4)
        mlp_total = backward_up(dy, pre_act, w_up_v, middle, gain_b_of(layer), middle, normed_low)
        if layer == 1:
            load(2, 0)
        run("middle")
        if layer == 0:
            restored(0)
            restored(2)
        turned[...] = conv[...].T
        if layer == 1:
            restore(0)
        rows_out = own[0][OUT].shape[1]
        for cols in blocks(hidden, COLS):
            out_put(OUT, cols.start // rows_out, out_part(cols, 1 - core))
        if layer == 0:
            restored(1)
            restored(3)
            loaded(1)

        def in_out(index):
            out_put(IN + index, 0, in_part(index, 1 - core))

        def in_own(index):
            own_put(layer, IN + index, 0, in_part(index, core))

        def in_send(index):
            free_first(layer, IN + index)
            send(layer, IN + index, 0)

        def gates(index):
            backward_gates(linked, normed_low, w_out_v, retain, states, slope, update, pre_act, index)

        gates(0)
        send_first(layer, OUT)
        run(0)
        in_out(0)
        gates(1)
        send_first(layer, IN)
        take_first(OUT)
        run(1)
        in_out(1)
        for cols in blocks(hidden, COLS):
            own_put(layer, OUT, cols.start // rows_out, out_part(cols, core))
        gates(2)
        send_first(layer, IN + 1)
        free_first(layer, OUT)
        send(layer, OUT, 0)
        take_first(IN)
        run(2)
        in_out(2)
        in_own(0)
        gates(3)
        send_first(layer, IN + 2)
        in_send(0)
        take_first(IN + 1)
        if layer == 1:
            for number in (1, 2, 3, 5):
                restore(number)
            load(1, 0)
        if layer == 0:
            loaded(0)
        run(3)
        in_out(3)
        in_own(1)
        send_first(layer, IN + 3)
        in_send(1)
        take_first(IN + 2)
        in_own(2)
        backward_conv(pre_act, w_in_v, normed)
        in_send(2)
        take_first(IN + 3)
        in_own(3)
        in_send(3)
        if layer == 1:
            restore(7)
            load(0, 0)
        run("in done")
        if layer == 0:
            restored(8)
        mix_total, tap_totals = backward_mix(linked, xb, gain_a_of(layer), taps_of(layer), middle, normed, dy)
        if layer == 1:
            restore(4)
            restore(8)
        totals = [mix_total] + tap_totals + [mlp_total]
        small[layer] = jnp.concatenate(
            [jnp.sum(total, axis=0, keepdims=True) for total in totals] + [jnp.zeros((2, width), f32)], axis=0
        )

    def second(unit):
        return -unit - 1

    backward(
        1,
        {
            0: [(DOWN, 0)],
            3: [(UP, 0)],
            "in done": [(DOWN, 1), (OUT, 0), (IN, 0)],
        },
    )
    published(stage_a, layer_out, 0, 0)
    swap_order(dy, stage_a)
    publish(stage_a, input_grads, 1, 2)
    step(1, IN + 1, 0)
    step(1, IN + 2, 0)
    step(1, UP, 1)
    backward(
        0,
        {
            "down sent": [(second(IN + 3), 0), (second(DOWN), 2)],
            "up sent": [(second(OUT), 1), (second(UP), 2), (second(IN), 1), (second(IN + 1), 1)],
            "down done": [(second(IN + 2), 1), (second(IN + 3), 1)],
            "up done": [(second(OUT), 2), (second(IN), 2), (second(IN + 1), 2), (second(DOWN), 3), (second(UP), 3)],
            "middle": [(second(OUT), 3), (second(IN), 3), (DOWN, 0), (second(IN + 1), 3), (second(IN + 2), 2), (second(IN + 3), 2)],
            2: [(UP, 0)],
            3: [(DOWN, 1), (second(IN + 2), 3), (second(IN + 3), 3)],
            "in done": [(OUT, 0), (IN, 0)],
        },
    )
    devices = [partner] + [place.across(stage) for stage in range(4)]

    def small_start(number):
        remote(small, small_land.at[number], small_sems.at[number], devices[number]).start()

    def small_take(number):
        remote(small, small_land.at[number], small_sems.at[number], devices[number]).wait()
        small[...] = small[...] + small_land[number]

    small_start(0)
    published(stage_b, layer_out, 1, 1)
    swap_order(dy, stage_b)
    publish(stage_b, input_grads, 0, 3)
    def late(steps):
        for unit, stage in steps:
            step(0, unit, stage)

    late([(DOWN, 2), (UP, 1)])
    small_take(0)
    small_start(1)
    late([(IN + 1, 0), (IN + 2, 0), (IN + 3, 0)])
    small_take(1)
    small_start(2)
    late([(OUT, 1), (IN, 1), (UP, 2), (DOWN, 3)])
    small_take(2)
    small_start(3)
    late([(OUT, 2), (IN, 2), (IN + 1, 1), (IN + 2, 1), (IN + 1, 2)])
    small_take(3)
    small_start(4)
    late([(IN + 3, 1), (IN + 2, 2), (UP, 3), (OUT, 3), (IN, 3), (IN + 3, 2), (IN + 1, 3), (IN + 2, 3), (IN + 3, 3)])
    small_take(4)
    if per_group == 1:
        lanes = width // GROUPS
        small_out[...] = pltpu.roll(small[core], lax.rem(width - place.index * lanes, width), 1)
    else:
        small_out[...] = small[core]

    published(stage_a, input_grads, 1, 2)
    published(stage_b, input_grads, 0, 3)
    for number in range(1, 4):
        remote(own_weights[number], far_weights[number], far_sems.at[number], partner).wait_send()
    for index in range(chunks):
        both = pl.ds(index * 2 * COLS, 2 * COLS)
        remote(own_weights[0].at[:, both], far_weights[0].at[:, both], chunk_sems.at[index], partner).wait_send()
    for layer in range(2):
        for unit in range(units):

            @pl.when(core == layer)
            def _():
                remote(result[unit], final_part(unit, 1 - core), last_sems.at[unit], partner).wait_recv()

            @pl.when(core != layer)
            def _():
                remote(result[unit], final_part(unit, core), last_sems.at[unit], partner).wait_send()


def train(per_group, inputs, joined, cotangent, gain_a, taps, w_in, w_out, gain_b, w_up, w_down):
    length, width = inputs.shape[2:]
    hidden, inner = w_out.shape[1], w_up.shape[2]
    batches = inputs.shape[0]
    shape = jax.ShapeDtypeStruct
    vmem, anywhere = pl.BlockSpec(memory_space=pltpu.VMEM), pl.BlockSpec(memory_space=pl.ANY)
    weights = (w_in, w_out, w_up, w_down)
    pieces = [(weight.shape[1] // GROUPS, weight.shape[2]) for weight in (w_down, w_up, w_out, w_in)]
    kept = [
        ((length, width), bf16),
        ((length, hidden), f32),
        ((length, hidden), f32),
        ((length, hidden), bf16),
        ((length, width), f32),
        ((length, width), bf16),
        ((length, inner), bf16),
        ((length, inner), bf16),
        ((length, width), bf16),
    ]
    outs = [shape((1, batches, 1, length, width), bf16)] * 2
    outs += [shape((1,) + pieces[piece], f32) for piece in (IN, OUT, UP, DOWN)]
    outs += [shape((8, width), f32)]
    spaces = [anywhere] * 2 + [vmem] * 5
    outs += [shape(weight.shape[1:], bf16) for weight in weights]
    outs += [shape(*entry) for entry in kept]
    spaces += [anywhere] * (len(outs) - len(spaces))

    def unit_buffers(count, kind):
        lead = (count,) if count else ()
        found = []
        for piece, chunk in UNITS:
            rows, columns = pieces[piece]
            found.append(pltpu.VMEM(lead + (rows, columns // 2 if chunk is None else COLS), kind))
        return found

    small_rows = pltpu.VMEM((8, width), f32)
    small_pair = pltpu.VMEM((2, 8, width), f32)
    dma, regular = pltpu.SemaphoreType.DMA, pltpu.SemaphoreType.REGULAR
    units, chunks = len(UNITS), hidden // COLS
    assert chunks == units - IN
    scratch = [pltpu.VMEM((length, width), bf16) for _ in range(4)]
    scratch += [pltpu.VMEM((width, length), bf16)]
    scratch += [pltpu.VMEM(*entry) for entry in kept[:8]]
    scratch += [pltpu.VMEM((length + 3 * GROUP, width), f32), pltpu.VMEM((2 * COLS // LANES, length, LANES), f32)]
    scratch += [pltpu.VMEM(weight.shape[1:], bf16) for weight in weights]
    scratch += [small_pair, small_rows, small_pair, pltpu.VMEM((5, 2, 8, width), f32)]
    scratch += unit_buffers(GROUPS, bf16) * 2 + unit_buffers(GROUPS, bf16)[:3] * 2
    for layer in range(2):
        for stage in range(layer, 4):
            scratch += unit_buffers(GROUPS >> (stage + 1), bf16)
    scratch += unit_buffers(0, f32)
    scratch += [dma((2,)), dma((4 + chunks,)), dma((chunks, 2)), dma((4,)), dma((len(kept),)), dma((4, 2)), dma((2,))]
    scratch += [dma((4, 2)), dma((units, 2)), dma((2, units, 4, 2)), dma((units, 2)), dma((5, 2))]
    scratch += [regular((3,)), regular((units,))]
    results = pl.pallas_call(
        lambda *refs: train_body(per_group, *refs),
        out_shape=outs,
        in_specs=[anywhere, vmem, anywhere, vmem, vmem, anywhere, anywhere, vmem, anywhere, anywhere],
        out_specs=spaces,
        scratch_shapes=scratch,
        compiler_params=pltpu.CompilerParams(vmem_limit_bytes=LIMIT, collective_id=0, has_side_effects=True),
        name="train",
    )(inputs, joined, cotangent, gain_a, taps, w_in, w_out, gain_b, w_up, w_down)
    return results[:7]


def write_body(*refs):
    sources, small, targets = refs[:6], refs[6], refs[7:13]
    gain_a, taps, gain_b, refs = refs[13], refs[14], refs[15], refs[16:]
    held, sems = refs[:6], refs[6]
    for number in range(6):
        pltpu.make_async_copy(sources[number], held[number], sems.at[0, number]).start()
    lanes = gain_a.shape[1]
    gain_a[...] = small[0:1, 0:lanes]
    taps[0] = small[1:5, 0:lanes]
    gain_b[...] = small[5:6, 0:lanes]
    for number in range(6):
        pltpu.make_async_copy(sources[number], held[number], sems.at[0, number]).wait()
        pltpu.make_async_copy(held[number], targets[number], sems.at[1, number]).start()
    for number in range(6):
        pltpu.make_async_copy(held[number], targets[number], sems.at[1, number]).wait()


def write_results(*args):
    arrays, small, lanes = args[:6], args[6], args[7]
    shape = jax.ShapeDtypeStruct
    vmem, outside = pl.BlockSpec(memory_space=pltpu.VMEM), pl.BlockSpec(memory_space=pltpu.HBM)
    outs = [shape(array.shape, array.dtype) for array in arrays]
    outs += [shape((1, lanes), f32), shape((1, 4, lanes), f32), shape((1, lanes), f32)]
    layer_out, input_grads, g_in, g_out, g_up, g_down, gain_a, taps, gain_b = pl.pallas_call(
        write_body,
        out_shape=outs,
        in_specs=[outside] * 6 + [vmem],
        out_specs=[outside] * 6 + [vmem] * 3,
        scratch_shapes=[pltpu.VMEM(array.shape, array.dtype) for array in arrays] + [pltpu.SemaphoreType.DMA((2, 6))],
        compiler_params=pltpu.CompilerParams(vmem_limit_bytes=LIMIT),
        name="write_results",
    )(*arrays, small)
    return (layer_out, input_grads, gain_a, taps, g_in, g_out, gain_b, g_up, g_down)


def local(inputs, joined, cotangent, gain_mix, conv_taps, w_in, w_out, gain_mlp, w_up, w_down):
    dp = lax.axis_size("dp")
    per_group = dp // GROUPS
    layer_out, input_grads, g_in, g_out, g_up, g_down, small = train(
        per_group, inputs, joined, cotangent, gain_mix, conv_taps, w_in, w_out, gain_mlp, w_up, w_down
    )
    if per_group > 1:
        members = [[group * per_group + inner for inner in range(per_group)] for group in range(GROUPS)]

        def finish(grad):
            return lax.psum_scatter(grad, "dp", scatter_dimension=1, axis_index_groups=members, tiled=True)

        g_in, g_out, g_up, g_down = [finish(grad) for grad in (g_in, g_out, g_up, g_down)]
        small = lax.psum(small, "dp", axis_index_groups=members)
    else:
        return write_results(layer_out, input_grads, g_in, g_out, g_up, g_down, small, small.shape[1] // dp)
    lanes = small.shape[1] // dp
    small = lax.dynamic_slice_in_dim(small, lax.axis_index("dp") * lanes, lanes, 1)
    return (layer_out, input_grads, small[0:1], small[None, 1:5], g_in, g_out, small[5:6], g_up, g_down)


def solution(mesh):
    placed = (
        P(None, "dp", None, None),
        P(None, "dp"),
        P(None, "dp", None, None),
        P("section", None),
        P("section", None, None),
        P("section", None, None),
        P("section", None, None),
        P("section", None),
        P("section", None, None),
        P("section", None, None),
    )
    return jax.shard_map(
        local,
        mesh=mesh,
        in_specs=placed,
        out_specs=(
            P("section", None, "dp", None, None),
            P("section", None, "dp", None, None),
            P("section", "dp"),
            P("section", None, "dp"),
            P("section", "dp", None),
            P("section", "dp", None),
            P("section", "dp"),
            P("section", "dp", None),
            P("section", "dp", None),
        ),
        check_vma=False,
    )
```

```python
import jax
import jax.numpy as jnp
from jax import lax
from jax.experimental import pallas as pl
from jax.experimental.pallas import tpu as pltpu
from jax.sharding import PartitionSpec as P

f32 = jnp.float32
bf16 = jnp.bfloat16
epsilon = 1e-06
GROUP = 32
COLS = 256
LANES = 128
GELU_A = 0.7978845608028654
GELU_B = GELU_A * 0.044715


def dot(left, right):
    return jnp.dot(left, right, preferred_element_type=f32)


def dot_nt(left, right):
    return lax.dot_general(left, right, (((1,), (1,)), ((), ())), preferred_element_type=f32)


def dot_tn(left, right):
    return lax.dot_general(left, right, (((0,), (0,)), ((), ())), preferred_element_type=f32)


def segment_rows(shape):
    return lax.broadcasted_iota(jnp.int32, shape, 0)


def entry_factor(shape, linked):
    row = segment_rows(shape)
    return jnp.where(row == 0, 0.0, jnp.where(row == GROUP // 2, linked, 1.0))


def exit_factor(shape, linked):
    row = segment_rows(shape)
    return jnp.where(row == GROUP - 1, 0.0, jnp.where(row == GROUP // 2 - 1, linked, 1.0))


def blocks(total, size):
    return [slice(start, start + size) for start in range(0, total, size)]


def inverse_norm(values):
    return lax.rsqrt(jnp.mean(values * values, axis=-1, keepdims=True) + epsilon)


def fold_rows(values):
    rows, width = values.shape
    return jnp.sum(values.reshape(rows // 8, 8, width), axis=0)


def logistic_pair(logit):
    away = jnp.exp(-jnp.maximum(logit, -80.0))
    opened = 1.0 / (1.0 + away)
    return opened, away * opened


def softplus_parts(value):
    small = jnp.exp(-jnp.abs(value))
    whole = 1.0 + small
    inverse = pltpu.reciprocal(whole, approx=True)
    log_part = jnp.where(small < 2.0**-10, small * (1.0 - 0.5 * small), jnp.log(whole))
    slope = jnp.where(value >= 0, inverse, small * inverse)
    return jnp.maximum(value, 0.0) + log_part, slope


def gelu_half(value, square):
    return 0.5 + 0.5 * jnp.tanh(value * (GELU_A + GELU_B * square))


def gelu(value):
    return value * gelu_half(value, value * value)


def gelu_slope(value):
    square = value * value
    half = gelu_half(value, square)
    return half * (1.0 + (1.0 - half) * (value * (2.0 * GELU_A + 6.0 * GELU_B * square)))


def swap_order(source, target):
    length, width = source.shape
    steps = length // GROUP
    assert steps == GROUP
    target[...] = jnp.swapaxes(source[...].reshape(steps, GROUP, width), 0, 1).reshape(length, width)


def forward_mix(linked, x, gain, taps, normed, conv):
    length, width = x.shape
    lead = 3 * GROUP
    for rows in blocks(length, 128):
        values = x[rows].astype(f32)
        normed[lead + rows.start : lead + rows.stop] = values * inverse_norm(values) * gain
    factor = entry_factor((GROUP, width), linked)
    for back in range(1, 4):
        start = lead + length - back * GROUP
        block = normed[start : start + GROUP]
        normed[lead - back * GROUP : lead - (back - 1) * GROUP] = pltpu.roll(block, 1, 0) * factor
    for rows in blocks(length, 128):
        total = normed[lead + rows.start : lead + rows.stop] * taps[0]
        for back in range(1, 4):
            start = lead - back * GROUP + rows.start
            total = total + normed[start : start + 128] * taps[back]
        conv[rows] = total.astype(bf16)


def forward_scan(linked, retain, update, states, states_low, cols):
    length = retain.shape[0]
    steps = length // GROUP
    shape = (GROUP, LANES)
    ends = update[0:GROUP]
    spans = retain[0:GROUP, cols]
    for step in range(1, steps):
        rows = slice(step * GROUP, (step + 1) * GROUP)
        keep = retain[rows, cols]
        ends = keep * ends + update[rows]
        spans = keep * spans
    factor = entry_factor(shape, linked)
    spans = spans * factor
    row = segment_rows(shape)
    distance = 1
    while distance < GROUP:
        reach = jnp.where(row >= distance, spans, 0.0)
        ends = ends + reach * pltpu.roll(ends, distance, 0)
        spans = reach * pltpu.roll(spans, distance, 0)
        distance = 2 * distance
    carry = pltpu.roll(ends, 1, 0) * factor
    for step in range(steps):
        rows = slice(step * GROUP, (step + 1) * GROUP)
        carry = retain[rows, cols] * carry + update[rows]
        states[rows, cols] = carry
        states_low[rows, cols] = carry.astype(bf16)


def forward_gates(linked, conv, w_in, retain, update, states, states_low, slope, index):
    hidden = states.shape[1]
    cols = slice(index * COLS, (index + 1) * COLS)
    far = slice(hidden + index * COLS, hidden + (index + 1) * COLS)
    opened, kept = logistic_pair(dot(conv[...], w_in[:, cols]))
    retain[:, cols] = kept
    soft, soft_slope = softplus_parts(dot(conv[...], w_in[:, far]))
    slope[:, cols] = (opened * soft_slope).astype(bf16)
    added = opened * soft
    for half in range(COLS // LANES):
        part = update.at[(index % 2) * (COLS // LANES) + half]
        part[...] = added[:, half * LANES : (half + 1) * LANES]
        lanes = slice(cols.start + half * LANES, cols.start + (half + 1) * LANES)
        forward_scan(linked, retain, part, states, states_low, lanes)


def forward_middle(x, states_low, w_out, gain, middle, normed_low):
    hidden = w_out.shape[0]
    for rows in blocks(x.shape[0], 256):
        values = x[rows].astype(f32) + dot(states_low[rows, 0:hidden], w_out[...])
        middle[rows] = values
        normed_low[rows] = (values * inverse_norm(values) * gain).astype(bf16)


def forward_up(normed_low, w_up, act, pre_act):
    for cols in blocks(act.shape[1], COLS):
        values = dot(normed_low[...], w_up[:, cols])
        act[:, cols] = gelu(values).astype(bf16)
        pre_act[:, cols] = values.astype(bf16)


def forward_down(middle, act, w_down, out):
    for rows in blocks(middle.shape[0], 256):
        out[rows] = (middle[rows] + dot(act[rows], w_down[...])).astype(bf16)


def backward_up(dy, d_pre, w_up, middle, gain, d_middle, d_middle_low):
    total = jnp.zeros((8, dy.shape[1]), f32)
    for rows in blocks(dy.shape[0], 256):
        d_normed = dot_nt(d_pre[rows], w_up[...])
        values = middle[rows]
        scale = inverse_norm(values)
        unit = values * scale
        total = total + fold_rows(d_normed * unit)
        d_unit = d_normed * gain
        mean = jnp.mean(d_unit * unit, axis=-1, keepdims=True)
        result = dy[rows].astype(f32) + scale * (d_unit - unit * mean)
        d_middle[rows] = result
        d_middle_low[rows] = result.astype(bf16)
    return total


def backward_scan(linked, retain, states, slope, d_states, d_proj, cols, far):
    length = retain.shape[0]
    steps = length // GROUP
    shape = (GROUP, LANES)
    last = slice(length - GROUP, length)
    running = d_states[last]
    spans = retain[last, cols]
    for step in range(steps - 2, -1, -1):
        rows = slice(step * GROUP, (step + 1) * GROUP)
        after = retain[(step + 1) * GROUP : (step + 2) * GROUP, cols]
        running = d_states[rows] + after * running
        spans = spans * retain[rows, cols]
    entry = entry_factor(shape, linked)
    ends = retain[0:GROUP, cols] * running * entry
    spans = spans * entry
    row = segment_rows(shape)
    distance = 1
    while distance < GROUP:
        reach = jnp.where(row < GROUP - distance, spans, 0.0)
        ends = ends + reach * pltpu.roll(ends, GROUP - distance, 0)
        spans = reach * pltpu.roll(spans, GROUP - distance, 0)
        distance = 2 * distance
    running = jnp.where(row < GROUP - 1, pltpu.roll(ends, GROUP - 1, 0), 0.0)
    first_before = pltpu.roll(states[last, cols], 1, 0) * entry
    for step in range(steps - 1, -1, -1):
        rows = slice(step * GROUP, (step + 1) * GROUP)
        running = d_states[rows] + running
        keep = retain[rows, cols]
        before = states[(step - 1) * GROUP : step * GROUP, cols] if step else first_before
        decayed = keep * running
        d_proj[rows, cols] = (decayed * (states[rows, cols] - before)).astype(bf16)
        d_proj[rows, far] = (running * slope[rows, cols].astype(f32)).astype(bf16)
        running = decayed


def backward_gates(linked, d_middle_low, w_out, retain, states, slope, d_states, d_proj, index):
    hidden = states.shape[1]
    cols = slice(index * COLS, (index + 1) * COLS)
    d_hidden = dot_nt(d_middle_low[...], w_out[cols])
    for half in range(COLS // LANES):
        part = d_states.at[(index % 2) * (COLS // LANES) + half]
        part[...] = d_hidden[:, half * LANES : (half + 1) * LANES]
        lanes = slice(cols.start + half * LANES, cols.start + (half + 1) * LANES)
        far = slice(hidden + lanes.start, hidden + lanes.stop)
        backward_scan(linked, retain, states, slope, part, d_proj, lanes, far)


def backward_conv(d_proj, w_in, d_conv):
    for rows in blocks(d_proj.shape[0], 256):
        d_conv[rows] = dot_nt(d_proj[rows], w_in[...])


def backward_mix(linked, x, gain, taps, d_middle, d_conv, out):
    length, width = x.shape
    factor = exit_factor((GROUP, width), linked)
    for ahead in range(3):
        block = d_conv[ahead * GROUP : (ahead + 1) * GROUP]
        d_conv[length + ahead * GROUP : length + (ahead + 1) * GROUP] = pltpu.roll(block, GROUP - 1, 0) * factor
    gain_total = jnp.zeros((8, width), f32)
    tap_totals = [jnp.zeros((8, width), f32) for _ in range(4)]
    for rows in blocks(length, 128):
        values = x[rows].astype(f32)
        scale = inverse_norm(values)
        unit = values * scale
        normed = unit * gain
        d_normed = jnp.zeros_like(unit)
        for ahead in range(4):
            shifted = d_conv[rows.start + ahead * GROUP : rows.stop + ahead * GROUP]
            tap_totals[ahead] = tap_totals[ahead] + fold_rows(normed * shifted)
            d_normed = d_normed + shifted * taps[ahead]
        gain_total = gain_total + fold_rows(d_normed * unit)
        d_unit = d_normed * gain
        mean = jnp.mean(d_unit * unit, axis=-1, keepdims=True)
        out[rows] = (d_middle[rows] + scale * (d_unit - unit * mean)).astype(bf16)
    return gain_total, tap_totals


MESH = pl.DeviceIdType.MESH
GROUPS = 16
LIMIT = 63 * 2**20 + 2**19
DOWN, UP, OUT, IN = range(4)
UNITS = ((DOWN, None), (UP, None), (OUT, None), (IN, 0), (IN, 1))


class Place:
    def __init__(self, per_group):
        self.core = lax.axis_index("section")
        self.index = lax.axis_index("dp")
        self.per_group = per_group
        self.inner = lax.rem(self.index, per_group)
        group = lax.div(self.index, per_group)
        low = lax.rem(group, 2)
        high = lax.rem(lax.div(group, 2), 2)
        near = lax.rem(lax.div(group, 4), 2)
        far = lax.div(group, 8)
        first = low + self.core * (high - low)
        third = high + self.core * (low - high)
        self.digits = (first, near, third, far)

    def group(self, digits):
        first, near, third, far = digits
        low = first + self.core * (third - first)
        high = third + self.core * (first - third)
        return far * 8 + near * 4 + high * 2 + low

    def other_core(self):
        return (1 - self.core, self.index)

    def across(self, stage):
        digits = list(self.digits)
        digits[stage] = 1 - digits[stage]
        return (self.core, self.group(digits) * self.per_group + self.inner)

    def position(self, group):
        low, high, near, far = group % 2, group // 2 % 2, group // 4 % 2, group // 8
        on_first = low * 8 + near * 4 + high * 2 + far
        on_second = high * 8 + near * 4 + low * 2 + far
        return on_first + self.core * (on_second - on_first)

    def range_of(self, stage, mine):
        start = sum(self.digits[before] * (8 >> before) for before in range(stage))
        digit = self.digits[stage]
        start = start + (digit if mine else 1 - digit) * (8 >> stage)
        return pl.ds(start, 8 >> stage)


def remote(source, target, sems, device):
    return pltpu.make_async_remote_copy(
        src_ref=source, dst_ref=target, send_sem=sems.at[0], recv_sem=sems.at[1], device_id=device, device_id_type=MESH
    )


def train_body(per_group, *refs):
    refs = list(refs)

    def take(count):
        taken = refs[:count]
        del refs[:count]
        return taken

    inputs, joined, cotangent, gain_a, taps, w_in, w_out, gain_b, w_up, w_down = take(10)
    layer_out, input_grads, g_in, g_out, g_up, g_down, small_out = take(7)
    far_weights = take(4)
    stored = take(9)
    xb, dy, stage_a, stage_b, turned, conv, retain, states, slope, middle, normed_low, act, pre_act, normed, update = take(15)
    weights = take(4)
    params, own_params, small, small_land = take(4)
    units = len(UNITS)
    own = [take(units), take(units)]
    out_first, in_first = take(3), take(3)
    landing = [[take(units) for _ in range(4)], [take(units) for _ in range(3)]]
    landing[1].insert(0, landing[0][0])
    result = take(units)
    in_sems, weight_sems, chunk_sems, spill_sems, store_sems, far_sems, param_sems, move_sems = take(8)
    first_sems, stage_sems, last_sems, small_sems, credits, stage_credits = take(6)
    assert not refs

    place = Place(per_group)
    core = place.core
    partner = place.other_core()
    linked = jnp.where(core == 0, joined[0:1, 0:1], joined[0:1, 1:2]).astype(f32)
    w_in_v, w_out_v, w_up_v, w_down_v = weights
    final = {DOWN: g_down, UP: g_up, OUT: g_out, IN: g_in}
    length, width = xb.shape
    hidden, inner = states.shape[1], act.shape[1]
    chunks = hidden // COLS

    barrier = pltpu.get_barrier_semaphore()
    greeted = [partner] + [place.across(stage) for stage in range(4)]
    for device in greeted:
        pl.semaphore_signal(barrier, inc=1, device_id=device, device_id_type=MESH)
    fetch_x = pltpu.make_async_copy(inputs.at[core, 0], stage_a, in_sems.at[0])
    fetch_x.start()
    fetch_dy = pltpu.make_async_copy(cotangent.at[core, 0], stage_b, in_sems.at[1])
    fetch_dy.start()
    own_params[...] = jnp.concatenate(
        [gain_a[...].astype(f32), taps[0].astype(f32), gain_b[...].astype(f32), jnp.zeros((2, width), f32)], axis=0
    )
    own_weights = [weight.at[0] for weight in (w_in, w_out, w_up, w_down)]

    def in_chunk(index):
        return [slice(side * hidden + index * COLS, side * hidden + (index + 1) * COLS) for side in range(2)]

    def load(number, layer):
        @pl.when(core == layer)
        def _():
            pltpu.make_async_copy(own_weights[number], weights[number], weight_sems.at[number]).start()

        @pl.when(core != layer)
        def _():
            pltpu.make_async_copy(far_weights[number], weights[number], weight_sems.at[number]).start()

    def loaded(number):
        pltpu.make_async_copy(own_weights[number], weights[number], weight_sems.at[number]).wait()

    def spill(number):
        @pl.when(core == 1)
        def _():
            pltpu.make_async_copy(weights[number], far_weights[number], spill_sems.at[number]).start()

    def load_second(number):
        @pl.when(core == 1)
        def _():
            pltpu.make_async_copy(weights[number], far_weights[number], spill_sems.at[number]).wait()

        @pl.when(core == 0)
        def _():
            if number:
                remote(own_weights[number], far_weights[number], far_sems.at[number], partner).wait_recv()
            else:
                for index in range(chunks):
                    both = pl.ds(index * 2 * COLS, 2 * COLS)
                    remote(own_weights[0].at[:, both], far_weights[0].at[:, both], chunk_sems.at[index], partner).wait_recv()

        load(number, 1)

    pl.semaphore_wait(barrier, len(greeted))
    to_params = remote(own_params, params.at[core], param_sems, partner)
    to_params.start()

    @pl.when(core == 0)
    def _():
        for index in range(chunks):
            for cols in in_chunk(index):
                pltpu.make_async_copy(own_weights[0].at[:, cols], w_in_v.at[:, cols], weight_sems.at[4 + index]).start()
        for index in range(chunks):
            for cols in in_chunk(index):
                remote(own_weights[0].at[:, cols], w_in_v.at[:, cols], chunk_sems.at[index], partner).start()
        for number in range(1, 4):
            pltpu.make_async_copy(own_weights[number], weights[number], weight_sems.at[number]).start()
            remote(own_weights[number], weights[number], far_sems.at[number], partner).start()

    @pl.when(core == 1)
    def _():
        for index in range(chunks):
            for cols in in_chunk(index):
                remote(own_weights[0].at[:, cols], far_weights[0].at[:, cols], chunk_sems.at[index], partner).start()
        for number in range(1, 4):
            remote(own_weights[number], far_weights[number], far_sems.at[number], partner).start()

    def loaded_first(number):
        @pl.when(core == 0)
        def _():
            loaded(number)

        @pl.when(core == 1)
        def _():
            remote(own_weights[number], weights[number], far_sems.at[number], partner).wait_recv()

        spill(number)

    def loaded_chunk(index):
        both = pl.ds(index * 2 * COLS, 2 * COLS)

        @pl.when(core == 0)
        def _():
            pltpu.make_async_copy(own_weights[0].at[:, both], w_in_v.at[:, both], weight_sems.at[4 + index]).wait()

        @pl.when(core == 1)
        def _():
            remote(own_weights[0].at[:, both], w_in_v.at[:, both], chunk_sems.at[index], partner).wait_recv()

    params[core] = own_params[...]

    def gain_a_of(layer):
        return params[layer, 0:1, :]

    def taps_of(layer):
        return [params[layer, 1 + tap : 2 + tap, :] for tap in range(4)]

    def gain_b_of(layer):
        return params[layer, 5:6, :]

    kept = (conv, retain, states, slope, middle, normed_low, act, pre_act, xb)

    def store(number):
        pltpu.make_async_copy(kept[number], stored[number], store_sems.at[number]).start()

    def stored_done(number):
        pltpu.make_async_copy(kept[number], stored[number], store_sems.at[number]).wait()

    def restore(number):
        pltpu.make_async_copy(stored[number], kept[number], store_sems.at[number]).start()

    def restored(number):
        pltpu.make_async_copy(stored[number], kept[number], store_sems.at[number]).wait()

    def publish(source, target, layer, number):
        @pl.when(core == layer)
        def _():
            pltpu.make_async_copy(source, target.at[0, core, 0], move_sems.at[number, 0]).start()

        @pl.when(core != layer)
        def _():
            remote(source, target.at[0, core, 0], move_sems.at[number], partner).start()

    def published(source, target, layer, number):
        @pl.when(core == layer)
        def _():
            pltpu.make_async_copy(source, target.at[0, core, 0], move_sems.at[number, 0]).wait()
            remote(source, target.at[0, 1 - core, 0], move_sems.at[number], partner).wait_recv()

        @pl.when(core != layer)
        def _():
            remote(source, target.at[0, core, 0], move_sems.at[number], partner).wait_send()

    fetch_x.wait()
    swap_order(stage_a, xb)
    store(8)
    to_params.wait()
    forward_mix(linked, xb, gain_a_of(0), taps_of(0), normed, conv)
    store(0)
    for index in range(chunks):
        loaded_chunk(index)
        forward_gates(linked, conv, w_in_v, retain, update, states, pre_act, slope, index)
    spill(0)
    for number in (1, 2, 3):
        store(number)
    loaded_first(1)
    forward_middle(xb, pre_act, w_out_v, gain_b_of(0), middle, normed_low)
    store(4)
    store(5)
    load_second(0)
    loaded_first(2)
    forward_up(normed_low, w_up_v, act, pre_act)
    load_second(1)
    store(7)
    store(6)
    stored_done(8)
    loaded_first(3)
    forward_down(middle, act, w_down_v, xb)
    load_second(2)

    swap_order(xb, stage_a)
    publish(stage_a, layer_out, 0, 0)
    stored_done(0)
    forward_mix(linked, xb, gain_a_of(1), taps_of(1), normed, conv)
    load_second(3)
    for number in (1, 2, 3, 7):
        stored_done(number)
    loaded(0)
    for index in range(chunks):
        forward_gates(linked, conv, w_in_v, retain, update, states, pre_act, slope, index)
    fetch_dy.wait()
    swap_order(stage_b, dy)
    stored_done(4)
    stored_done(5)
    loaded(1)
    forward_middle(xb, pre_act, w_out_v, gain_b_of(1), middle, normed_low)
    stored_done(6)
    loaded(2)
    loaded(3)

    def half_of(piece, which):
        size = 2 * width // 4 if piece in (DOWN, OUT) else inner // 2
        return pl.ds(pl.multiple_of(which * size, size), size)

    def within(piece, chunk):
        return slice(None) if chunk is None else slice(chunk * 2 * COLS, (chunk + 1) * 2 * COLS)

    def first_refs(unit):
        piece, chunk = UNITS[unit]
        place_of = UP if piece == IN else piece
        cols = within(piece, chunk)
        return out_first[place_of].at[:, :, cols], in_first[place_of].at[:, :, cols]

    def send_first(layer, unit):
        piece, chunk = UNITS[unit]
        if (layer == 0 and piece != IN) or chunk == 0:
            pl.semaphore_wait(credits.at[UP if piece == IN else piece], 1)
        remote(*first_refs(unit), first_sems.at[unit], partner).start()

    def take_first(unit):
        remote(*first_refs(unit), first_sems.at[unit], partner).wait()

    def free_first(layer, unit):
        piece, chunk = UNITS[unit]
        if piece == UP or (layer == 1 and chunk in (None, 1)):
            pl.semaphore_signal(credits.at[UP if piece == IN else piece], inc=1, device_id=partner, device_id_type=MESH)

    def send(layer, unit, stage):
        if layer == 0 and stage == 0:
            pl.semaphore_wait(stage_credits.at[unit], 1)
        source = own[layer][unit].at[place.range_of(stage, False)]
        remote(source, landing[layer][stage][unit], stage_sems.at[layer, unit, stage], place.across(stage)).start()

    def step(layer, unit, stage):
        mine, land = own[layer][unit].at[place.range_of(stage, True)], landing[layer][stage][unit]
        remote(mine, land, stage_sems.at[layer, unit, stage], place.across(stage)).wait()
        if stage < 3:
            mine[...] = mine[...] + land[...]
            if layer == 1 and stage == 0:
                pl.semaphore_signal(stage_credits.at[unit], inc=1, device_id=place.across(0), device_id_type=MESH)
            send(layer, unit, stage + 1)
            return
        total = mine[0].astype(f32) + land[0].astype(f32)
        target = final_part(unit, core)

        @pl.when(core == layer)
        def _():
            target[...] = total

        @pl.when(core != layer)
        def _():
            result[unit][...] = total
            remote(result[unit], target, last_sems.at[unit], partner).start()

    def final_part(unit, which):
        piece, chunk = UNITS[unit]
        if chunk is None:
            return final[piece].at[0, :, half_of(piece, which)]
        return final[piece].at[0, :, pl.ds(pl.multiple_of(which * hidden + chunk * 2 * COLS, COLS), 2 * COLS)]

    def own_put(layer, unit, first_group, values, cols=slice(None)):
        rows = own[layer][unit].shape[1]
        landed = first_refs(unit)[1]
        for number in range(values.shape[0] // rows):
            group = first_group + number
            total = values[number * rows : (number + 1) * rows] + landed[group, :, cols].astype(f32)
            own[layer][unit][place.position(group), :, cols] = total.astype(bf16)

    def out_put(unit, first_group, values, cols=slice(None)):
        target = first_refs(unit)[0]
        rows = target.shape[1]
        count = values.shape[0] // rows
        target[first_group : first_group + count, :, cols] = values.astype(bf16).reshape(count, rows, values.shape[1])

    def backward(layer, plan):
        def run(point):
            for unit, stage in plan.get(point, ()):
                if unit < 0:
                    step(1, -unit - 1, stage)
                else:
                    step(layer, unit, stage)

        def down_part(cols, which):
            return dot_tn(act[:, cols], dy[:, half_of(DOWN, which)])

        def d_pre_part(which, offset):
            start = which * (inner // 2) + offset
            cols = pl.ds(pl.multiple_of(start, COLS), COLS)
            d_act = dot_nt(dy[...], w_down_v[cols, :])
            values = (d_act * gelu_slope(pre_act[:, cols].astype(f32))).astype(bf16)
            pre_act[:, cols] = values
            return dot(turned[...], values)

        def out_part(cols, which):
            return dot_tn(states[:, cols].astype(bf16), normed_low[:, half_of(OUT, which)])

        def in_part(index, which):
            cols = pl.ds(pl.multiple_of(which * hidden + index * COLS, COLS), COLS)
            return dot(turned[...], pre_act[:, cols])

        rows_down = own[0][DOWN].shape[1]
        if layer == 1:
            forward_up(normed_low, w_up_v, act, pre_act)
        else:
            restored(6)
            restored(5)
        for cols in blocks(inner, COLS):
            out_put(DOWN, cols.start // rows_down, down_part(cols, 1 - core))
        turned[...] = normed_low[...].T
        send_first(layer, DOWN)
        run("down sent")
        if layer == 0:
            restored(7)
            loaded(3)
        for offset in range(0, inner // 2, COLS):
            out_put(UP, 0, d_pre_part(1 - core, offset), slice(offset, offset + COLS))
        send_first(layer, UP)
        run("up sent")
        take_first(DOWN)
        for cols in blocks(inner, COLS):
            own_put(layer, DOWN, cols.start // rows_down, down_part(cols, core))
        free_first(layer, DOWN)
        send(layer, DOWN, 0)
        if layer == 1:
            forward_down(middle, act, w_down_v, stage_b)
            swap_order(stage_b, stage_b)
            publish(stage_b, layer_out, 1, 1)
            restore(6)
        else:
            published(stage_a, layer_out, 0, 0)
            swap_order(dy, stage_a)
            publish(stage_a, input_grads, 1, 2)
        run("down done")
        take_first(UP)
        for offset in range(0, inner // 2, COLS):
            own_put(layer, UP, 0, d_pre_part(core, offset), slice(offset, offset + COLS))
        free_first(layer, UP)
        send(layer, UP, 0)
        if layer == 1:
            load(3, 0)
        run("up done")
        if layer == 0:
            loaded(2)
            restored(4)
        mlp_total = backward_up(dy, pre_act, w_up_v, middle, gain_b_of(layer), middle, normed_low)
        if layer == 1:
            load(2, 0)
        run("middle")
        if layer == 0:
            restored(0)
            restored(2)
        turned[...] = conv[...].T
        if layer == 1:
            restore(0)
        rows_out = own[0][OUT].shape[1]
        for cols in blocks(hidden, COLS):
            out_put(OUT, cols.start // rows_out, out_part(cols, 1 - core))
        if layer == 0:
            restored(1)
            restored(3)
            loaded(1)

        def in_half(index):
            return IN + index // 2, slice(index % 2 * COLS, (index % 2 + 1) * COLS)

        def in_out(index):
            unit, cols = in_half(index)
            out_put(unit, 0, in_part(index, 1 - core), cols)

        def in_own(index):
            unit, cols = in_half(index)
            own_put(layer, unit, 0, in_part(index, core), cols)

        def in_send(unit):
            free_first(layer, unit)
            send(layer, unit, 0)

        def gates(index):
            backward_gates(linked, normed_low, w_out_v, retain, states, slope, update, pre_act, index)

        gates(0)
        send_first(layer, OUT)
        run(0)
        in_out(0)
        gates(1)
        take_first(OUT)
        run(1)
        in_out(1)
        for cols in blocks(hidden, COLS):
            own_put(layer, OUT, cols.start // rows_out, out_part(cols, core))
        gates(2)
        send_first(layer, IN)
        free_first(layer, OUT)
        send(layer, OUT, 0)
        run(2)
        in_out(2)
        gates(3)
        take_first(IN)
        if layer == 1:
            for number in (1, 2, 3, 5):
                restore(number)
            load(1, 0)
        if layer == 0:
            loaded(0)
        run(3)
        in_out(3)
        send_first(layer, IN + 1)
        in_own(0)
        in_own(1)
        in_send(IN)
        run("in half")
        if layer == 1:
            backward_conv(pre_act, w_in_v, normed)
        take_first(IN + 1)
        in_own(2)
        in_own(3)
        in_send(IN + 1)
        if layer == 1:
            restore(7)
            load(0, 0)
        run("in done")
        if layer == 0:
            backward_conv(pre_act, w_in_v, normed)
            run("conv")
        if layer == 0:
            restored(8)
        mix_total, tap_totals = backward_mix(linked, xb, gain_a_of(layer), taps_of(layer), middle, normed, dy)
        run("mix")
        if layer == 1:
            restore(4)
            restore(8)
        totals = [mix_total] + tap_totals + [mlp_total]
        small[layer] = jnp.concatenate(
            [jnp.sum(total, axis=0, keepdims=True) for total in totals] + [jnp.zeros((2, width), f32)], axis=0
        )

    def second(unit):
        return -unit - 1

    backward(
        1,
        {
            "middle": [(DOWN, 0)],
            2: [(UP, 0)],
            3: [(DOWN, 1)],
            "in done": [(OUT, 0), (DOWN, 2)],
            "mix": [(UP, 1), (IN, 0)],
        },
    )
    backward(
        0,
        {
            "down sent": [(second(IN + 1), 0), (second(OUT), 1)],
            "up sent": [(second(DOWN), 3), (second(UP), 2), (second(OUT), 2), (second(IN), 1)],
            "down done": [(second(IN + 1), 1)],
            "up done": [(second(IN), 2), (second(UP), 3), (second(OUT), 3)],
            "middle": [(DOWN, 0), (second(IN), 3), (second(IN + 1), 2)],
            2: [(UP, 0)],
            3: [(DOWN, 1), (second(IN + 1), 3)],
            "in done": [(OUT, 0), (DOWN, 2)],
            "conv": [(UP, 1), (IN, 0)],
            "mix": [(OUT, 1), (IN + 1, 0), (DOWN, 3), (UP, 2)],
        },
    )
    devices = [partner] + [place.across(stage) for stage in range(4)]

    def small_start(number):
        remote(small, small_land.at[number], small_sems.at[number], devices[number]).start()

    def small_take(number):
        remote(small, small_land.at[number], small_sems.at[number], devices[number]).wait()
        small[...] = small[...] + small_land[number]

    small_start(0)
    published(stage_b, layer_out, 1, 1)
    swap_order(dy, stage_b)
    publish(stage_b, input_grads, 0, 3)
    def late(steps):
        for unit, stage in steps:
            step(0, unit, stage)

    small_take(0)
    small_start(1)
    late([(OUT, 2), (IN, 1)])
    small_take(1)
    small_start(2)
    late([(IN + 1, 1), (IN, 2), (UP, 3)])
    small_take(2)
    small_start(3)
    late([(OUT, 3), (IN + 1, 2), (IN, 3)])
    small_take(3)
    small_start(4)
    late([(IN + 1, 3)])
    small_take(4)
    if per_group == 1:
        lanes = width // GROUPS
        small_out[...] = pltpu.roll(small[core], lax.rem(width - place.index * lanes, width), 1)
    else:
        small_out[...] = small[core]

    published(stage_a, input_grads, 1, 2)
    published(stage_b, input_grads, 0, 3)
    for number in range(1, 4):
        remote(own_weights[number], far_weights[number], far_sems.at[number], partner).wait_send()
    for index in range(chunks):
        both = pl.ds(index * 2 * COLS, 2 * COLS)
        remote(own_weights[0].at[:, both], far_weights[0].at[:, both], chunk_sems.at[index], partner).wait_send()
    for layer in range(2):
        for unit in range(units):

            @pl.when(core == layer)
            def _():
                remote(result[unit], final_part(unit, 1 - core), last_sems.at[unit], partner).wait_recv()

            @pl.when(core != layer)
            def _():
                remote(result[unit], final_part(unit, core), last_sems.at[unit], partner).wait_send()


def train(per_group, inputs, joined, cotangent, gain_a, taps, w_in, w_out, gain_b, w_up, w_down):
    length, width = inputs.shape[2:]
    hidden, inner = w_out.shape[1], w_up.shape[2]
    batches = inputs.shape[0]
    shape = jax.ShapeDtypeStruct
    vmem, anywhere = pl.BlockSpec(memory_space=pltpu.VMEM), pl.BlockSpec(memory_space=pl.ANY)
    weights = (w_in, w_out, w_up, w_down)
    pieces = [(weight.shape[1] // GROUPS, weight.shape[2]) for weight in (w_down, w_up, w_out, w_in)]
    kept = [
        ((length, width), bf16),
        ((length, hidden), f32),
        ((length, hidden), f32),
        ((length, hidden), bf16),
        ((length, width), f32),
        ((length, width), bf16),
        ((length, inner), bf16),
        ((length, inner), bf16),
        ((length, width), bf16),
    ]
    outs = [shape((1, batches, 1, length, width), bf16)] * 2
    outs += [shape((1,) + pieces[piece], f32) for piece in (IN, OUT, UP, DOWN)]
    outs += [shape((8, width), f32)]
    spaces = [anywhere] * 2 + [vmem] * 5
    outs += [shape(weight.shape[1:], bf16) for weight in weights]
    outs += [shape(*entry) for entry in kept]
    spaces += [anywhere] * (len(outs) - len(spaces))

    def unit_buffers(count, kind):
        lead = (count,) if count else ()
        found = []
        for piece, chunk in UNITS:
            rows, columns = pieces[piece]
            found.append(pltpu.VMEM(lead + (rows, columns // 2 if chunk is None else 2 * COLS), kind))
        return found

    small_rows = pltpu.VMEM((8, width), f32)
    small_pair = pltpu.VMEM((2, 8, width), f32)
    dma, regular = pltpu.SemaphoreType.DMA, pltpu.SemaphoreType.REGULAR
    units, chunks = len(UNITS), hidden // COLS
    assert chunks == 4
    scratch = [pltpu.VMEM((length, width), bf16) for _ in range(4)]
    scratch += [pltpu.VMEM((width, length), bf16)]
    scratch += [pltpu.VMEM(*entry) for entry in kept[:8]]
    scratch += [pltpu.VMEM((length + 3 * GROUP, width), f32), pltpu.VMEM((2 * COLS // LANES, length, LANES), f32)]
    scratch += [pltpu.VMEM(weight.shape[1:], bf16) for weight in weights]
    scratch += [small_pair, small_rows, small_pair, pltpu.VMEM((5, 2, 8, width), f32)]
    scratch += unit_buffers(GROUPS, bf16) * 2 + unit_buffers(GROUPS, bf16)[:3] * 2
    for layer in range(2):
        for stage in range(layer, 4):
            scratch += unit_buffers(GROUPS >> (stage + 1), bf16)
    scratch += unit_buffers(0, f32)
    scratch += [dma((2,)), dma((4 + chunks,)), dma((chunks, 2)), dma((4,)), dma((len(kept),)), dma((4, 2)), dma((2,))]
    scratch += [dma((4, 2)), dma((units, 2)), dma((2, units, 4, 2)), dma((units, 2)), dma((5, 2))]
    scratch += [regular((3,)), regular((units,))]
    results = pl.pallas_call(
        lambda *refs: train_body(per_group, *refs),
        out_shape=outs,
        in_specs=[anywhere, vmem, anywhere, vmem, vmem, anywhere, anywhere, vmem, anywhere, anywhere],
        out_specs=spaces,
        scratch_shapes=scratch,
        compiler_params=pltpu.CompilerParams(vmem_limit_bytes=LIMIT, collective_id=0, has_side_effects=True),
        name="train",
    )(inputs, joined, cotangent, gain_a, taps, w_in, w_out, gain_b, w_up, w_down)
    return results[:7]


def write_body(*refs):
    sources, small, targets = refs[:6], refs[6], refs[7:13]
    gain_a, taps, gain_b, refs = refs[13], refs[14], refs[15], refs[16:]
    held, sems = refs[:6], refs[6]
    reads, writes = [], []
    for number in range(6):
        reads.append(pltpu.make_async_copy(sources[number], held[number], sems.at[0, number]))
        writes.append(pltpu.make_async_copy(held[number], targets[number], sems.at[1, number]))
        reads[-1].start()
    lanes = gain_a.shape[1]
    gain_a[...] = small[0:1, 0:lanes]
    taps[0] = small[1:5, 0:lanes]
    gain_b[...] = small[5:6, 0:lanes]
    for read, write in zip(reads, writes):
        read.wait()
        write.start()
    for write in writes:
        write.wait()


def write_results(*args):
    arrays, small, lanes = args[:6], args[6], args[7]
    shape = jax.ShapeDtypeStruct
    vmem, outside = pl.BlockSpec(memory_space=pltpu.VMEM), pl.BlockSpec(memory_space=pltpu.HBM)
    outs = [shape(array.shape, array.dtype) for array in arrays]
    outs += [shape((1, lanes), f32), shape((1, 4, lanes), f32), shape((1, lanes), f32)]
    layer_out, input_grads, g_in, g_out, g_up, g_down, gain_a, taps, gain_b = pl.pallas_call(
        write_body,
        out_shape=outs,
        in_specs=[outside] * 6 + [vmem],
        out_specs=[outside] * 6 + [vmem] * 3,
        scratch_shapes=[pltpu.VMEM(array.shape, array.dtype) for array in arrays] + [pltpu.SemaphoreType.DMA((2, 6))],
        compiler_params=pltpu.CompilerParams(vmem_limit_bytes=LIMIT),
        name="write_results",
    )(*arrays, small)
    return (layer_out, input_grads, gain_a, taps, g_in, g_out, gain_b, g_up, g_down)


def local(inputs, joined, cotangent, gain_mix, conv_taps, w_in, w_out, gain_mlp, w_up, w_down):
    dp = lax.axis_size("dp")
    per_group = dp // GROUPS
    layer_out, input_grads, g_in, g_out, g_up, g_down, small = train(
        per_group, inputs, joined.T, cotangent, gain_mix, conv_taps, w_in, w_out, gain_mlp, w_up, w_down
    )
    if per_group > 1:
        members = [[group * per_group + inner for inner in range(per_group)] for group in range(GROUPS)]

        def finish(grad):
            return lax.psum_scatter(grad, "dp", scatter_dimension=1, axis_index_groups=members, tiled=True)

        g_in, g_out, g_up, g_down = [finish(grad) for grad in (g_in, g_out, g_up, g_down)]
        small = lax.psum(small, "dp", axis_index_groups=members)
    else:
        return write_results(layer_out, input_grads, g_in, g_out, g_up, g_down, small, small.shape[1] // dp)
    lanes = small.shape[1] // dp
    small = lax.dynamic_slice_in_dim(small, lax.axis_index("dp") * lanes, lanes, 1)
    return (layer_out, input_grads, small[0:1], small[None, 1:5], g_in, g_out, small[5:6], g_up, g_down)


def solution(mesh):
    placed = (
        P(None, "dp", None, None),
        P(None, "dp"),
        P(None, "dp", None, None),
        P("section", None),
        P("section", None, None),
        P("section", None, None),
        P("section", None, None),
        P("section", None),
        P("section", None, None),
        P("section", None, None),
    )
    return jax.shard_map(
        local,
        mesh=mesh,
        in_specs=placed,
        out_specs=(
            P("section", None, "dp", None, None),
            P("section", None, "dp", None, None),
            P("section", "dp"),
            P("section", None, "dp"),
            P("section", "dp", None),
            P("section", "dp", None),
            P("section", "dp"),
            P("section", "dp", None),
            P("section", "dp", None),
        ),
        check_vma=False,
    )
```
